128 devices in a mesh: dp: 32 (over y, z, core), mp: 4 (over x).
Axes of the slice: x: 4, y: 4, z: 4, core: 2. Of those that a mesh axis runs over, the one named last changes fastest.
Arguments:
- queries: bfloat16 [7168, 2560], P('dp', 'mp'), may hold values from -7 to 7
- keys: bfloat16 [7168, 512], P('dp', 'mp'), may hold values from -7 to 7
- values: bfloat16 [7168, 512], P('dp', 'mp'), may hold values from -6 to 6
- seg_ids: int32 [7168], P('dp'), may hold values from 0 to 7, never falling along the last dimension, each value on 1 to 3584 neighbouring positions
- out_weight: bfloat16 [2560, 5120], P('mp'), may hold values from -0.125 to 0.125
- grad_out: bfloat16 [7168, 5120], P('dp', 'mp'), may hold values from -6 to 6
Outputs:
- projected: bfloat16 [7168, 5120], P('dp', 'mp')
- grad_query: bfloat16 [7168, 2560], P('dp', 'mp')
- grad_key: bfloat16 [7168, 512], P('dp', 'mp')
- grad_value: bfloat16 [7168, 512], P('dp', 'mp')
The draws below stay inside these ranges and needn't reach their ends.
Inputs may be any that keep to these rules, and one draw needn't show every extreme that they name: `seg_ids`: never falling along the tokens; 8 sequences of 1 to 3584 tokens, the longest exactly 3584.
All inputs are finite; a program needn't handle non-finite values.
Results may differ from the reference program's by a relative error of at most 0.011.
Values may be sent and summed in bfloat16 or wider, within the bound.
No kernel may reach another device: no remote copies, remote signals or barrier semaphores. Data moves between devices by JAX's collectives and lax.ppermute only.
A program may use at most 128 MiB of HBM per device.

```python
import math
import jax
import jax.numpy as jnp
import numpy as np
from jax import lax

D = 5120
HD = 128
QH = 20
KVH = 4
SEQS = 8
TOKENS = 7168


def draw_keys(key, part):
    key = jax.random.fold_in(key, 2)
    result = jax.random.truncated_normal(key, -5.0, 5.0, (TOKENS, KVH, HD))
    return result.astype(jnp.float32).reshape(TOKENS, KVH * HD).astype(jnp.bfloat16)


def draw_queries(key, part):
    key = jax.random.fold_in(key, 3)
    group = QH // KVH
    result = jax.random.truncated_normal(key, -5.0, 5.0, (TOKENS, KVH, group, HD))
    return result.astype(jnp.float32).reshape(TOKENS, QH * HD).astype(jnp.bfloat16)


def level_of(stream_key, shape, shards, smallest, high):
    def one(position, shards_of):
        steps = jax.random.uniform(jax.random.fold_in(jax.random.fold_in(stream_key, 6), position), (shards_of,), jnp.float32, smallest / len(shards), high / len(shards))
        return jnp.repeat(jnp.exp(steps), shape[position] // shards_of).reshape((-1,) + (1,) * (len(shape) - position - 1))

    level = one(*shards[0])
    for cut in shards[1:]:
        level = level * one(*cut)
    return level


def profile(count, total, most, slope):
    weights = [(1 << 20) // math.isqrt(rank ** slope) + 1 for rank in range(2, count + 1)]
    spare, holding = total - most - (count - 1), [1] * (count - 1)
    while spare > 0:
        free = [i for i in range(count - 1) if holding[i] < most]
        pool, left = sum([weights[i] for i in free]), spare
        for i in free:
            extra = min(most - holding[i], max(1, left * weights[i] // pool), spare)
            holding[i] = holding[i] + extra
            spare = spare - extra
    return np.array([most] + holding)


def ragged_sizes(key, number_of, total, reach, lean):
    if number_of == 2:
        one = jax.random.randint(key, (), max(1, total - reach), min(reach, total - 1) + 1)
        return jnp.stack([one, total - one])
    sizes = jnp.asarray(profile(number_of, total, reach, lean), jnp.int32)
    pairs = (number_of - 1) // 2
    source_of, receiver = sizes[1:1 + 2 * pairs:2], sizes[2:2 + 2 * pairs:2]
    margin = jnp.minimum(source_of - 1, reach - receiver)
    shifted = jax.random.randint(jax.random.fold_in(key, 1), (pairs,), 0, 1 << 20) % (margin + 1)
    sizes = sizes.at[1:1 + 2 * pairs:2].set(source_of - shifted).at[2:2 + 2 * pairs:2].set(receiver + shifted)
    return sizes[jax.random.permutation(jax.random.fold_in(key, 2), number_of)]


def bell_draw(rng, dims, scale, bound, cuts=(), kind=jnp.bfloat16):
    level = level_of(rng, dims, cuts, -0.22, 0.18) if cuts else 1.0
    values = jax.random.normal(rng, dims, jnp.float32) * scale * level
    return jnp.minimum(jnp.maximum(values, -bound), bound).astype(kind)


def setup_inputs(seed: int = 0) -> dict:
    streams_of = jax.random.split(jax.random.key(seed), 7)
    queries = draw_queries(jax.random.fold_in(streams_of[6], 71), 0)
    keys = draw_keys(jax.random.fold_in(streams_of[6], 71), 0)
    values = bell_draw(streams_of[2], (TOKENS, KVH * HD), 1.0, 6.0, ((0, 32), (1, 4)))
    seg_ids = jnp.searchsorted(jnp.cumsum(ragged_sizes(streams_of[3], SEQS, TOKENS, TOKENS // 2, 2)), jnp.arange(TOKENS), side="right").astype(jnp.int32)
    out_weight = bell_draw(streams_of[4], (QH * HD, D), (QH * HD) ** -0.5, 0.125, ((0, 4),))
    grad_out = bell_draw(streams_of[5], (TOKENS, D), 1.0, 6.0, ((0, 32), (1, 4)))
    return dict(queries=queries, keys=keys, values=values, seg_ids=seg_ids, out_weight=out_weight, grad_out=grad_out)


NEGATIVE = -1e+30

def reference(queries, keys, values, seg_ids, out_weight, grad_out):
    group = QH // KVH
    scale = 1.0 / math.sqrt(HD)
    block = math.gcd(TOKENS, 512)
    blocks = TOKENS // block
    positions = jnp.arange(TOKENS, dtype=jnp.int32)
    highest = lax.Precision.HIGHEST
    d_attn = jnp.dot(grad_out, out_weight.T, preferred_element_type=jnp.float32).astype(jnp.bfloat16)

    def head_pass(head):
        key_head = lax.dynamic_slice_in_dim(keys, head * HD, HD, 1).astype(jnp.float32)
        value_head = lax.dynamic_slice_in_dim(values, head * HD, HD, 1).astype(jnp.float32)
        query_heads = lax.dynamic_slice_in_dim(queries, head * group * HD, group * HD, 1).reshape(TOKENS, group, HD)
        grad_heads = lax.dynamic_slice_in_dim(d_attn, head * group * HD, group * HD, 1).reshape(TOKENS, group, HD)

        def step(carry, index):
            key_acc, value_acc = carry
            start = (index * block).astype(jnp.int32)
            query_part = lax.dynamic_slice_in_dim(query_heads, start, block, 0).astype(jnp.float32)
            grad_part = lax.dynamic_slice_in_dim(grad_heads, start, block, 0).astype(jnp.float32)
            row_ids = start + jnp.arange(block, dtype=jnp.int32)
            row_segs = lax.dynamic_slice_in_dim(seg_ids, start, block, 0)
            visible = (row_segs[:, None] == seg_ids[None, :]) & (positions[None, :] <= row_ids[:, None])
            scores = jnp.einsum('rhd,sd->hrs', query_part, key_head, precision=highest) * scale
            scores = jnp.where(visible[None], scores, NEGATIVE)
            peak = lax.optimization_barrier(jnp.max(scores, axis=2, keepdims=True))
            total = lax.optimization_barrier(jnp.sum(jnp.where(visible[None], jnp.exp(scores - peak), 0.0), axis=2, keepdims=True))
            lse = peak + jnp.log(total)
            weights = jnp.where(visible[None], jnp.exp(scores - lse), 0.0)
            rounded = weights.astype(jnp.bfloat16).astype(jnp.float32)
            attn_part = jnp.einsum('hrs,sd->rhd', rounded, value_head, precision=highest).astype(jnp.bfloat16)
            delta = lax.optimization_barrier(jnp.sum(grad_part * attn_part.astype(jnp.float32), axis=2))
            dprob = jnp.einsum('rhd,sd->hrs', grad_part, value_head, precision=highest)
            score_grad = (weights * (dprob - delta.T[:, :, None])).astype(jnp.bfloat16).astype(jnp.float32)
            query_grad = (jnp.einsum('hrs,sd->rhd', score_grad, key_head, precision=highest) * scale).astype(jnp.bfloat16)
            key_acc = key_acc + jnp.einsum('hrs,rhd->sd', score_grad, query_part, precision=highest)
            value_acc = value_acc + jnp.einsum('hrs,rhd->sd', rounded, grad_part, precision=highest)
            return ((key_acc, value_acc), (attn_part, query_grad))
        zeros = jnp.zeros((TOKENS, HD), jnp.float32)
        (key_acc, value_acc), (attn_parts, query_grads) = lax.scan(step, (zeros, zeros), jnp.arange(blocks, dtype=jnp.int32))
        return (attn_parts.reshape(TOKENS, group * HD), query_grads.reshape(TOKENS, group * HD), (key_acc * scale).astype(jnp.bfloat16), value_acc.astype(jnp.bfloat16))
    attn_all, query_all, key_all, value_all = lax.map(head_pass, jnp.arange(KVH, dtype=jnp.int32))
    attn = jnp.transpose(attn_all, (1, 0, 2)).reshape(TOKENS, QH * HD)
    grad_query = jnp.transpose(query_all, (1, 0, 2)).reshape(TOKENS, QH * HD)
    grad_key = jnp.transpose(key_all, (1, 0, 2)).reshape(TOKENS, KVH * HD)
    grad_value = jnp.transpose(value_all, (1, 0, 2)).reshape(TOKENS, KVH * HD)
    projected = jnp.dot(attn, out_weight, preferred_element_type=jnp.float32).astype(jnp.bfloat16)
    return (projected, grad_query, grad_key, grad_value)
```

```python
import math

import jax
import jax.numpy as jnp
from jax import lax
from jax.experimental import pallas as pl
from jax.experimental.pallas import tpu as pltpu
from jax.sharding import PartitionSpec as P

HD = 128
GROUP = 5
NZ = 4
NY = 4
REACH = 2
TILE = 16
LOW = -1e30
HIGH = 1e30
F32 = jnp.float32
BF16 = jnp.bfloat16
NT = (((1,), (1,)), ((), ()))
TN = (((0,), (0,)), ((), ()))
NN = (((1,), (0,)), ((), ()))


def place(y, z, core):
    return ((y % NY) * NZ + (z % NZ)) * 2 + core


def shift(dy, dz, flip):
    pairs = []
    for y in range(NY):
        for z in range(NZ):
            for core in range(2):
                if 0 <= y + dy < NY:
                    pairs.append((place(y, z, core), place(y + dy, z + dz, core ^ flip)))
    return pairs


def move(value, dy=0, dz=0, flip=0):
    return lax.ppermute(value, "dp", shift(dy, dz, flip))


def dot(a, b, dims):
    return lax.dot_general(a, b, dims, preferred_element_type=F32)


def where_am_i():
    index = lax.axis_index("dp")
    return index // (2 * NZ), (index // 2) % NZ, index % 2


def copies(near, near_other, far, far_other, kv, sem):
    y, z, core = where_am_i()
    started = []
    for back in range(NZ):
        source_z = lax.rem(z + NZ - back, NZ)
        for flip, near_ref, far_ref in ((0, near, far), (1, near_other, far_other)):
            col = source_z * 2 + (core if flip == 0 else 1 - core)
            started.append((near_ref.at[back], kv.at[REACH * 2 * NZ + col]))
            for dy in range(1, REACH + 1):
                started.append((far_ref.at[back, dy - 1], kv.at[(REACH - dy) * 2 * NZ + col]))
    return [pltpu.make_async_copy(s, d, sem.at[i]) for i, (s, d) in enumerate(started)]


def stack_heads(source, target, rows):
    for head in range(GROUP):
        target[head * rows : (head + 1) * rows, :] = source[:, head * HD : (head + 1) * HD]
    target[GROUP * rows :, :] = jnp.zeros((target.shape[0] - GROUP * rows, HD), BF16)


def forward_kernel(rows, factor, seg0, info, q, near, near_o, far, far_o, attn, attn_t, lse, prior_out, kv, q5, top, total, acc, sem):
    started = copies(near, near_o, far, far_o, kv, sem)
    for copy in started:
        copy.start()
    stack_heads(q, q5, rows)
    y, z, core = where_am_i()
    mine = REACH * 2 * NZ + z * 2 + core
    first = (REACH - y) * 2 * NZ
    for copy in started:
        copy.wait()
    seg = seg0[0].astype(F32)

    def count(slot, so_far):
        tile = kv[slot, rows:, :].astype(F32)
        return so_far + jnp.where(tile == seg, 1.0, 0.0)

    counted = lax.fori_loop(jnp.maximum(first, 0), mine, count, jnp.zeros((TILE, 2 * HD), F32))
    prior = jnp.sum(counted).astype(jnp.int32)
    prior_out[0] = prior
    row_pos = info[0:1, :]
    row_start = info[1:2, :]
    row_near = info[2:3, :] > 0.5
    width = info.shape[1]
    key_pos = lax.broadcasted_iota(jnp.int32, (rows, width), 0)

    key = kv[mine, :rows, :HD]
    value = kv[mine, :rows, HD:]
    scores = dot(key, q5[...], NT) * factor
    key_f = key_pos.astype(F32)
    scores = jnp.where((key_f <= row_pos) & (key_f >= row_start), scores, LOW)
    peak = jnp.max(scores, axis=0, keepdims=True)
    p = jnp.exp2(scores - peak)
    top[...] = peak
    total[...] = jnp.sum(p, axis=0, keepdims=True)
    acc[...] = dot(value, p.astype(BF16), TN)

    def step(slot, _):
        key = kv[slot, :rows, :HD]
        value = kv[slot, :rows, HD:]
        begin = (mine - slot) * rows - prior
        scores = dot(key, q5[...], NT) * factor
        scores = jnp.where(key_pos >= begin, scores, LOW)
        peak = jnp.max(scores, axis=0, keepdims=True)
        old = top[...]
        new = jnp.maximum(old, jnp.where(row_near, peak, LOW))
        top[...] = new
        alpha = jnp.exp2(old - new)
        p = jnp.exp2(scores - jnp.where(row_near, new, HIGH))
        total[...] = total[...] * alpha + jnp.sum(p, axis=0, keepdims=True)
        acc[...] = acc[...] * alpha + dot(value, p.astype(BF16), TN)
        return 0

    low = jnp.maximum(mine - (prior + rows - 1) // rows, 0)
    lax.fori_loop(low, mine, step, 0)
    out_t = (acc[...] / total[...]).astype(BF16)
    attn_t[...] = out_t
    lse[...] = top[...] + jnp.log2(total[...])
    out = out_t.T
    for head in range(GROUP):
        attn[:, head * HD : (head + 1) * HD] = out[head * rows : (head + 1) * rows, :]


def backward_kernel(rows, factor, scale, prior_in, info, q, grad, attn_t, lse, near, near_o, far, far_o, dq, stay, leave, kv, q5, g5, acc, sem):
    started = copies(near, near_o, far, far_o, kv, sem)
    for copy in started:
        copy.start()
    stack_heads(q, q5, rows)
    stack_heads(grad, g5, rows)
    stay[...] = jnp.zeros(stay.shape, BF16)
    leave[...] = jnp.zeros(leave.shape, BF16)
    y, z, core = where_am_i()
    mine = REACH * 2 * NZ + z * 2 + core
    prior = prior_in[0]
    row_pos = info[0:1, :]
    row_start = info[1:2, :]
    row_near = info[2:3, :] > 0.5
    width = info.shape[1]
    key_pos = lax.broadcasted_iota(jnp.int32, (rows, width), 0)
    delta = jnp.sum(attn_t[...].astype(F32) * g5[...].T.astype(F32), axis=0, keepdims=True)
    for copy in started:
        copy.wait()

    def block(slot, visible, norm):
        key = kv[slot, :rows, :HD]
        value = kv[slot, :rows, HD:]
        scores = dot(key, q5[...], NT) * factor
        p = jnp.where(visible, jnp.exp2(scores - norm), 0.0)
        slope = (p * (dot(value, g5[...], NT) - delta)).astype(BF16)
        d_value = dot(p.astype(BF16), g5[...], NN).astype(BF16)
        d_key = (dot(slope, q5[...], NN) * scale).astype(BF16)
        depth = REACH - slot // (2 * NZ)
        slot_z = (slot // 2) % NZ
        away = lax.rem(slot_z + NZ - z, NZ)
        same = slot % 2 == core

        @pl.when(same)
        def _():
            stay[away, depth, :, :HD] = d_key
            stay[away, depth, :, HD:] = d_value

        @pl.when(jnp.logical_not(same))
        def _():
            leave[away, depth, :, :HD] = d_key
            leave[away, depth, :, HD:] = d_value

        return dot(key, slope, TN)

    key_f = key_pos.astype(F32)
    acc[...] = block(mine, (key_f <= row_pos) & (key_f >= row_start), lse[...])
    norm = jnp.where(row_near, lse[...], HIGH)

    def step(slot, _):
        begin = (mine - slot) * rows - prior
        acc[...] += block(slot, key_pos >= begin, norm)
        return 0

    low = jnp.maximum(mine - (prior + rows - 1) // rows, 0)
    lax.fori_loop(low, mine, step, 0)
    out = (acc[...] * scale).astype(BF16).T
    for head in range(GROUP):
        dq[:, head * HD : (head + 1) * HD] = out[head * rows : (head + 1) * rows, :]


def gather_keys(keys, values, seg_ids):
    rows = keys.shape[0]
    segs = jnp.pad(seg_ids.astype(BF16)[None, :], ((0, TILE - 1), (0, 2 * HD - rows)), constant_values=-1)
    own = jnp.concatenate([jnp.concatenate([keys, values], axis=1), segs], axis=0)
    behind = jnp.stack([move(own, dy=dy) for dy in range(1, REACH + 1)])
    near = jnp.stack([own] + [move(own, dz=dz) for dz in range(1, NZ)])
    near_other = move(near, flip=1)
    far = jnp.stack([behind] + [move(behind, dz=dz) for dz in range(1, NZ)])
    far_other = move(far, flip=1)
    return near, near_other, far, far_other


def add_up(*terms):
    return sum(t.astype(F32) for t in terms)


def return_grads(stay, leave):
    mixed = add_up(stay, move(leave, flip=1)).astype(BF16)
    column = add_up(mixed[0], *[move(mixed[dz], dz=dz) for dz in range(1, NZ)])
    rounded = column.astype(BF16)
    return add_up(column[0], *[move(rounded[dy], dy=-dy) for dy in range(1, REACH + 1)]).astype(BF16)


def row_info(seg_ids, width):
    rows = seg_ids.shape[0]
    position = jnp.arange(rows, dtype=F32)
    start = jnp.sum(seg_ids[None, :] < seg_ids[:, None], axis=1).astype(F32)
    near = (seg_ids == seg_ids[0]).astype(F32)
    info = jnp.stack([position, start, near] + [jnp.zeros(rows, F32)] * 5)
    info = jnp.tile(info, (1, GROUP))
    return jnp.concatenate([info, jnp.tile(info[:, -1:], (1, width - GROUP * rows))], axis=1)


def per_device(queries, keys, values, seg_ids, out_weight, grad_out):
    rows = queries.shape[0]
    scale = 1.0 / math.sqrt(HD)
    factor = scale * math.log2(math.e)
    width = -(-GROUP * rows // 128) * 128
    slots = (REACH + 1) * 2 * NZ
    pieces = gather_keys(keys, values, seg_ids)
    info = row_info(seg_ids, width)
    any_spec = pl.BlockSpec(memory_space=pl.ANY)
    vmem = pl.BlockSpec(memory_space=pltpu.VMEM)
    smem = pl.BlockSpec(memory_space=pltpu.SMEM)
    params = pltpu.CompilerParams(vmem_limit_bytes=56 * 1024 * 1024)
    kv_scratch = pltpu.VMEM((slots, rows + TILE, 2 * HD), BF16)
    stacked = pltpu.VMEM((width, HD), BF16)
    attn, attn_t, lse, prior = pl.pallas_call(
        lambda *refs: forward_kernel(rows, factor, *refs),
        out_shape=(
            jax.ShapeDtypeStruct((rows, GROUP * HD), BF16),
            jax.ShapeDtypeStruct((HD, width), BF16),
            jax.ShapeDtypeStruct((1, width), F32),
            jax.ShapeDtypeStruct((1,), jnp.int32),
        ),
        in_specs=[smem, vmem, vmem] + [any_spec] * 4,
        out_specs=(vmem, vmem, vmem, smem),
        scratch_shapes=[
            kv_scratch,
            stacked,
            pltpu.VMEM((1, width), F32),
            pltpu.VMEM((1, width), F32),
            pltpu.VMEM((HD, width), F32),
            pltpu.SemaphoreType.DMA((slots,)),
        ],
        compiler_params=params,
    )(seg_ids[:1], info, queries, *pieces)
    term = jnp.dot(attn, out_weight, preferred_element_type=F32).astype(BF16)
    projected = lax.psum_scatter(term, "mp", scatter_dimension=1, tiled=True)
    d_attn = lax.dot_general(
        lax.all_gather(grad_out, "mp", axis=1, tiled=True),
        out_weight,
        NT,
        preferred_element_type=F32,
    ).astype(BF16)
    grads = jax.ShapeDtypeStruct((NZ, REACH + 1, rows, 2 * HD), BF16)
    grad_query, stay, leave = pl.pallas_call(
        lambda *refs: backward_kernel(rows, factor, scale, *refs),
        out_shape=(jax.ShapeDtypeStruct((rows, GROUP * HD), BF16), grads, grads),
        in_specs=[smem] + [vmem] * 5 + [any_spec] * 4,
        out_specs=(vmem, vmem, vmem),
        scratch_shapes=[
            kv_scratch,
            stacked,
            stacked,
            pltpu.VMEM((HD, width), F32),
            pltpu.SemaphoreType.DMA((slots,)),
        ],
        compiler_params=params,
    )(prior, info, queries, d_attn, attn_t, lse, *pieces)
    own = return_grads(stay, leave)
    return (projected, grad_query, own[:, :HD], own[:, HD:])


def solution(mesh):
    return jax.shard_map(
        per_device,
        mesh=mesh,
        in_specs=(
            P("dp", "mp"),
            P("dp", "mp"),
            P("dp", "mp"),
            P("dp"),
            P("mp", None),
            P("dp", "mp"),
        ),
        out_specs=(P("dp", "mp"), P("dp", "mp"), P("dp", "mp"), P("dp", "mp")),
        check_vma=False,
    )
```

```python
import math

import jax
import jax.numpy as jnp
from jax import lax
from jax.experimental import pallas as pl
from jax.experimental.pallas import tpu as pltpu
from jax.sharding import PartitionSpec as P

HD = 128
GROUP = 5
NX = 4
NY = 4
NZ = 4
TILE = 16
LOW = -1e30
HIGH = 1e30
F32 = jnp.float32
BF16 = jnp.bfloat16
NT = (((1,), (1,)), ((), ()))
TN = (((0,), (0,)), ((), ()))
NN = (((1,), (0,)), ((), ()))


def place(y, z, core):
    return ((y % NY) * NZ + (z % NZ)) * 2 + core


def shift(dy, dz, flip):
    pairs = []
    for y in range(NY):
        for z in range(NZ):
            for core in range(2):
                if 0 <= y + dy < NY:
                    pairs.append((place(y, z, core), place(y + dy, z + dz, core ^ flip)))
    return pairs


def move(value, dy=0, dz=0, flip=0):
    return lax.ppermute(value, "dp", shift(dy, dz, flip))


def move_x(value, dx):
    return lax.ppermute(value, "mp", [(x, (x + dx) % NX) for x in range(NX)])


def dot(a, b, dims):
    return lax.dot_general(a, b, dims, preferred_element_type=F32)


def where_am_i():
    index = lax.axis_index("dp")
    return index // (2 * NZ), (index // 2) % NZ, index % 2


def stack_heads(source, target, rows):
    for head in range(GROUP):
        target[head * rows : (head + 1) * rows, :] = source[:, head * HD : (head + 1) * HD]
    target[GROUP * rows :, :] = jnp.zeros((target.shape[0] - GROUP * rows, HD), BF16)


def spread_heads(stacked, target, rows):
    for head in range(GROUP):
        target[:, head * HD : (head + 1) * HD] = stacked[head * rows : (head + 1) * rows, :]


def joined(parts):
    return parts[0] if len(parts) == 1 else jnp.concatenate(parts, axis=0)


def seen(tile, seg, allowed, rows):
    count = jnp.sum(jnp.where(tile.astype(F32) == seg, 1.0, 0.0))
    return (rows - jnp.where(allowed, count, 0.0)).astype(jnp.int32)


def masks(refs, seg, core, info, rows, width, own):
    at = lax.broadcasted_iota(jnp.int32, (rows, width), 0)
    result = []
    for index, (ref, slot) in enumerate(refs):
        if own and index == 0:
            where = at.astype(F32)
            result.append((where <= info[0:1, :]) & (where >= info[1:2, :]))
        else:
            allowed = core == 1 if own and index == 1 else True
            result.append(at >= seen(ref[slot][rows:, :], seg, allowed, rows))
    return result


def attend(refs, visible, norm_of, q5, rows, factor, state, seen_rows):
    keys = joined([ref[slot][:rows, :HD] for ref, slot in refs])
    values = joined([ref[slot][:rows, HD:] for ref, slot in refs])
    raw = dot(keys, q5, NT)
    scores = [jnp.where(see, raw[i * rows : (i + 1) * rows], LOW) for i, see in enumerate(visible)]
    peak = jnp.max(scores[0], axis=0, keepdims=True)
    for part in scores[1:]:
        peak = jnp.maximum(peak, jnp.max(part, axis=0, keepdims=True))
    peak = peak * factor
    if seen_rows is not None:
        peak = jnp.where(seen_rows, peak, LOW)
    top, total, acc = state
    new = peak if top is None else jnp.maximum(top, peak)
    norm = new if seen_rows is None else jnp.where(seen_rows, new, HIGH)
    weights = [jnp.exp2(part * factor - norm) for part in scores]
    added = sum(jnp.sum(w, axis=0, keepdims=True) for w in weights)
    out = dot(values, joined([w.astype(BF16) for w in weights]), TN)
    if top is None:
        return new, added, out
    alpha = jnp.exp2(top - new)
    return new, total * alpha + added, acc * alpha + out


def column_refs(column, other):
    return [(column, 0), (other, 0), (column, 1), (other, 1), (column, 2), (other, 2)]


def side_refs(side, other, dz):
    return [(side, dz * 2), (other, dz * 2), (side, dz * 2 + 1), (other, dz * 2 + 1)]


def forward_column(rows, factor, seg0, info, q, column, other, top, total, acc, q5):
    stack_heads(q, q5, rows)
    _, _, core = where_am_i()
    width = info.shape[1]
    seg = seg0[0].astype(F32)
    near = info[2:3, :] > 0.5
    refs = column_refs(column, other)
    visible = masks(refs, seg, core, info, rows, width, True)
    state = attend(refs[:1], visible[:1], None, q5[...], rows, factor, (None, None, None), None)
    state = attend(refs[1:], visible[1:], None, q5[...], rows, factor, state, near)
    top[...], total[...], acc[...] = state


def forward_side(
    rows, factor, seg0, weight, info, q5, g5, side, other, top, total, acc,
    lse, delta, here, up, down, far_top, far_end, held, attn, sem,
):
    copy = pltpu.make_async_copy(weight, held, sem)
    copy.start()
    x = lax.axis_index("mp")
    _, _, core = where_am_i()
    width = info.shape[1]
    seg = seg0[0].astype(F32)
    near = info[2:3, :] > 0.5
    state = (top[...], total[...], acc[...])
    for dz in range(NZ - 1):
        refs = side_refs(side, other, dz)
        visible = masks(refs, seg, core, info, rows, width, False)
        state = attend(refs, visible, None, q5[...], rows, factor, state, near)
    out_t = (state[2] / state[1]).astype(BF16)
    spread_heads(out_t.T, attn, rows)
    lse[...] = state[0] + jnp.log2(state[1])
    delta[...] = jnp.sum(out_t.astype(F32) * g5[...].T.astype(F32), axis=0, keepdims=True)
    copy.wait()
    part = here.shape[1]

    def features(dx):
        column = pl.multiple_of(lax.rem(x + dx, NX) * part, 128)
        return dot(attn[...], held[:, pl.ds(column, part)], NN).astype(BF16)

    far = features(2)
    far_top[...] = far[: rows // 2]
    far_end[...] = far[rows // 2 :]
    up[...] = features(1)
    down[...] = features(3)
    here[...] = features(0)


def grads_of(refs, visible, norm, delta, q5, g5, rows, factor, scale):
    keys = joined([ref[slot][:rows, :HD] for ref, slot in refs])
    values = joined([ref[slot][:rows, HD:] for ref, slot in refs])
    raw = dot(keys, q5, NT)
    slope = dot(values, g5, NT)
    weights = []
    for i, see in enumerate(visible):
        part = raw[i * rows : (i + 1) * rows] * factor - norm
        weights.append(jnp.exp2(jnp.where(see, part, LOW)))
    weights = joined(weights)
    slope = (weights * (slope - delta)).astype(BF16)
    d_value = dot(weights.astype(BF16), g5, NN).astype(BF16)
    d_key = (dot(slope, q5, NN) * scale).astype(BF16)
    return d_key, d_value, dot(keys, slope, TN)


def backward_side(rows, factor, scale, parts, seg0, info, q5, g5, lse, delta, side, other, *rest):
    *before, acc, stay, leave = rest
    _, _, core = where_am_i()
    width = info.shape[1]
    seg = seg0[0].astype(F32)
    norm = jnp.where(info[2:3, :] > 0.5, lse[...], HIGH)
    total = before[0][...] if before else None
    for place_out, dz in enumerate(parts):
        refs = side_refs(side, other, dz - 1)
        visible = masks(refs, seg, core, info, rows, width, False)
        d_key, d_value, d_query = grads_of(refs, visible, norm, delta[...], q5[...], g5[...], rows, factor, scale)
        for i, (out, kind) in enumerate(((stay, 0), (leave, 0), (stay, 1), (leave, 1))):
            out[place_out, kind, :, :HD] = d_key[i * rows : (i + 1) * rows]
            out[place_out, kind, :, HD:] = d_value[i * rows : (i + 1) * rows]
        total = d_query if total is None else total + d_query
    acc[...] = total


def backward_column(rows, factor, scale, seg0, info, q5, g5, lse, delta, column, other, acc, dq, stay, leave):
    _, _, core = where_am_i()
    width = info.shape[1]
    seg = seg0[0].astype(F32)
    norm = jnp.where(info[2:3, :] > 0.5, lse[...], HIGH)
    refs = column_refs(column, other)
    outs = ((stay, 0), (leave, 0), (stay, 1), (leave, 1), (stay, 2), (leave, 2))
    visible = masks(refs, seg, core, info, rows, width, True)
    total = acc[...]
    for part, limit in ((slice(0, 1), lse[...]), (slice(1, 6), norm)):
        d_key, d_value, d_query = grads_of(
            refs[part], visible[part], limit, delta[...], q5[...], g5[...], rows, factor, scale
        )
        for i, (out, kind) in enumerate(outs[part]):
            out[kind, :, :HD] = d_key[i * rows : (i + 1) * rows]
            out[kind, :, HD:] = d_value[i * rows : (i + 1) * rows]
        total = total + d_query
    spread_heads((total * scale).astype(BF16).T, dq, rows)


def grad_heads(g0, g1, g2_top, g2_end, g3, weight, g5, held, weights, sem):
    x = lax.axis_index("mp")
    _, rows, part = held.shape
    half = rows // 2
    order = (0, 1, 3, 2)
    columns = [pl.multiple_of(lax.rem(x + NX - back, NX) * part, 128) for back in range(NX)]
    loads = [
        pltpu.make_async_copy(weight.at[:, pl.ds(columns[back], part)], weights.at[back], sem.at[back])
        for back in order
    ]
    pieces = (
        (g0, held.at[0]),
        (g1, held.at[1]),
        (g3, held.at[3]),
        (g2_top, held.at[2, pl.ds(0, half)]),
        (g2_end, held.at[2, pl.ds(half, half)]),
    )
    copies = [pltpu.make_async_copy(src, dst, sem.at[NX + i]) for i, (src, dst) in enumerate(pieces)]
    for copy in (loads[0], copies[0], loads[1], copies[1], loads[2], copies[2], loads[3], copies[3], copies[4]):
        copy.start()
    total = None
    for i, back in enumerate(order):
        loads[i].wait()
        copies[i].wait()
        if back == 2:
            copies[4].wait()
        term = dot(held[back], weights[back], NT)
        total = term if total is None else total + term
    stack_heads(total.astype(BF16), g5, rows)


def add_up(*terms):
    return sum(t.astype(F32) for t in terms)


def row_info(seg_ids, width):
    rows = seg_ids.shape[0]
    position = jnp.arange(rows, dtype=F32)
    start = jnp.sum(seg_ids[None, :] < seg_ids[:, None], axis=1).astype(F32)
    near = (seg_ids == seg_ids[0]).astype(F32)
    info = jnp.stack([position, start, near] + [jnp.zeros(rows, F32)] * 5)
    info = jnp.tile(info, (1, GROUP))
    return jnp.concatenate([info, jnp.tile(info[:, -1:], (1, width - GROUP * rows))], axis=1)


def per_device(queries, keys, values, seg_ids, out_weight, grad_out):
    rows = queries.shape[0]
    scale = 1.0 / math.sqrt(HD)
    factor = scale * math.log2(math.e)
    width = -(-GROUP * rows // 128) * 128
    _, z, _ = where_am_i()
    x = lax.axis_index("mp")
    vmem = pl.BlockSpec(memory_space=pltpu.VMEM)
    smem = pl.BlockSpec(memory_space=pltpu.SMEM)

    def shape(*dims, dtype=BF16):
        return jax.ShapeDtypeStruct(dims, dtype)

    anywhere = pl.BlockSpec(memory_space=pl.ANY)

    fixed = pl.BlockSpec(memory_space=pltpu.HBM)

    def call(body, outs, micros, *operands, scalars=1, loose=0, pinned=0, scratch=(), mib=24):
        return pl.pallas_call(
            body,
            out_shape=outs,
            in_specs=[smem] * scalars
            + [anywhere] * loose
            + [fixed] * pinned
            + [vmem] * (len(operands) - scalars - loose - pinned),
            out_specs=jax.tree.map(lambda _: vmem, outs),
            scratch_shapes=scratch,
            cost_estimate=pl.CostEstimate(flops=micros * 1_153_000_000, bytes_accessed=0, transcendentals=0),
            compiler_params=pltpu.CompilerParams(vmem_limit_bytes=mib * 1024 * 1024),
        )(*operands)

    line = shape(1, width, dtype=F32)
    square = shape(HD, width, dtype=F32)
    stacked = shape(width, HD)
    half = rows // 2

    segs = jnp.pad(
        (seg_ids + 1).astype(BF16)[None, :], ((0, TILE - 1), (0, 2 * HD - rows)), constant_values=0
    )
    seg0 = seg_ids[:1] + 1
    info = row_info(seg_ids, width)
    own = jnp.concatenate([jnp.concatenate([keys, values], axis=1), segs], axis=0)
    y1, y2 = move(own, dy=1), move(own, dy=2)
    g1, g3 = move_x(grad_out, 1), move_x(grad_out, 3)
    y1, y2, g1, g3 = lax.optimization_barrier((y1, y2, g1, g3))

    column = jnp.stack([own, y1, y2])
    column_other = move(column, flip=1)
    sides = [None] * (NZ - 1)
    for dz in (2, 1, 3):
        sides[dz - 1] = move(jnp.stack([y1, jnp.where(z + dz < NZ, own, y2)]), dz=dz)
    g2_top, g2_end = move_x(g1[:half], 1), move_x(g3[half:], 3)
    top, total, acc, q5 = call(
        lambda *refs: forward_column(rows, factor, *refs),
        (line, line, square, stacked), 3, seg0, info, queries, column, column_other,
    )
    *sides, g2_top, g2_end, top = lax.optimization_barrier((*sides, g2_top, g2_end, top))

    side = jnp.concatenate(sides)
    side_other = move(side, flip=1)
    part = grad_out.shape[1]
    g5 = call(
        grad_heads, stacked, 4, grad_out, g1, g2_top, g2_end, g3, out_weight, scalars=0, loose=5, pinned=1,
        scratch=[
            pltpu.VMEM((NX, rows, part), BF16),
            pltpu.VMEM((NX, out_weight.shape[0], part), BF16),
            pltpu.SemaphoreType.DMA((NX + 5,)),
        ],
    )
    whole, halved = shape(rows, part), shape(half, part)
    lse, delta, here, up, down, *far = call(
        lambda *refs: forward_side(rows, factor, *refs),
        (line, line, whole, whole, whole, halved, halved), 8,
        seg0, out_weight, info, q5, g5, side, side_other, top, total, acc, pinned=1, mib=30,
        scratch=[
            pltpu.VMEM(out_weight.shape, BF16),
            pltpu.VMEM((rows, GROUP * HD), BF16),
            pltpu.SemaphoreType.DMA,
        ],
    )
    early = (move_x(far[0], 1), move_x(far[1], 3))

    def side_grads(parts, micros, *before):
        pieces = shape(len(parts), 2, rows, 2 * HD)
        return call(
            lambda *refs: backward_side(rows, factor, scale, parts, *refs),
            (square, pieces, pieces), micros, seg0, info, q5, g5, lse, delta, side, side_other, *before,
        )

    acc, stay, leave, *early = lax.optimization_barrier((*side_grads((2, 1), 6), *early))
    up = jnp.concatenate([add_up(up[:half], early[0]).astype(BF16), up[half:]], axis=0)
    down = jnp.concatenate([down[:half], add_up(down[half:], early[1]).astype(BF16)], axis=0)
    other = move(leave, flip=1)
    acc, stay_last, leave_last, other = lax.optimization_barrier((*side_grads((3,), 3, acc), other))
    other_last = move(leave_last, flip=1)
    mixed = add_up(stay, other).astype(BF16)
    returned = {2: move(mixed[0], dz=-2), 1: move(mixed[1], dz=-1)}
    returned[3] = move(add_up(stay_last[0], other_last[0]).astype(BF16), dz=-3)
    column_grads = shape(3, rows, 2 * HD)
    up, down = move_x(up, 1), move_x(down, 3)
    grad_query, stay, leave, returned[1], returned[2], returned[3], up, down = lax.optimization_barrier(
        (
            *call(
                lambda *refs: backward_column(rows, factor, scale, *refs),
                (shape(rows, GROUP * HD), column_grads, column_grads), 5,
                seg0, info, q5, g5, lse, delta, column, column_other, acc,
            ),
            returned[1], returned[2], returned[3], up, down,
        )
    )
    projected = add_up(here, up, down).astype(BF16)
    mixed = add_up(stay, move(leave, flip=1))
    first, second, third = mixed[0], mixed[1], mixed[2]
    for dz in range(1, NZ):
        far, near = returned[dz][0].astype(F32), returned[dz][1].astype(F32)
        second = second + far
        first = first + jnp.where(z + dz < NZ, near, 0.0)
        third = third + jnp.where(z + dz < NZ, 0.0, near)
    second, third = second.astype(BF16), third.astype(BF16)
    grads = add_up(first, move(second, dy=-1), move(third, dy=-2)).astype(BF16)
    return (projected, grad_query, grads[:, :HD], grads[:, HD:])


def solution(mesh):
    return jax.shard_map(
        per_device,
        mesh=mesh,
        in_specs=(
            P("dp", "mp"),
            P("dp", "mp"),
            P("dp", "mp"),
            P("dp"),
            P("mp", None),
            P("dp", "mp"),
        ),
        out_specs=(P("dp", "mp"), P("dp", "mp"), P("dp", "mp"), P("dp", "mp")),
        check_vma=False,
    )
```

```python
import math

import jax
import jax.numpy as jnp
from jax import lax
from jax.experimental import pallas as pl
from jax.experimental.pallas import tpu as pltpu
from jax.sharding import PartitionSpec as P

HD = 128
GROUP = 5
NX = 4
NY = 4
NZ = 4
TILE = 16
LOW = -1e30
HIGH = 1e30
F32 = jnp.float32
BF16 = jnp.bfloat16
NT = (((1,), (1,)), ((), ()))
TN = (((0,), (0,)), ((), ()))
NN = (((1,), (0,)), ((), ()))


def place(y, z, core):
    return ((y % NY) * NZ + (z % NZ)) * 2 + core


def shift(dy, dz, flip):
    pairs = []
    for y in range(NY):
        for z in range(NZ):
            for core in range(2):
                pairs.append((place(y, z, core), place(y + dy, z + dz, core ^ flip)))
    return pairs


def move(value, dy=0, dz=0, flip=0):
    return lax.ppermute(value, "dp", shift(dy, dz, flip))


def move_x(value, dx):
    return lax.ppermute(value, "mp", [(x, (x + dx) % NX) for x in range(NX)])


def dot(a, b, dims):
    return lax.dot_general(a, b, dims, preferred_element_type=F32)


def where_am_i():
    index = lax.axis_index("dp")
    return index // (2 * NZ), (index // 2) % NZ, index % 2


def stack_heads(source, target, rows):
    for head in range(GROUP):
        target[head * rows : (head + 1) * rows, :] = source[:, head * HD : (head + 1) * HD]
    target[GROUP * rows :, :] = jnp.zeros((target.shape[0] - GROUP * rows, HD), BF16)


def spread_heads(stacked, target, rows):
    for head in range(GROUP):
        target[:, head * HD : (head + 1) * HD] = stacked[head * rows : (head + 1) * rows, :]


def joined(parts):
    return parts[0] if len(parts) == 1 else jnp.concatenate(parts, axis=0)


def seen(tile, seg, rows):
    count = jnp.sum(jnp.where(tile.astype(F32) == seg, 1.0, 0.0))
    return rows - count.astype(jnp.int32)


def masks(refs, info, rows, width, own):
    at = lax.broadcasted_iota(jnp.int32, (rows, width), 0)
    result = []
    for index, (ref, slot) in enumerate(refs):
        if own and index == 0:
            segs = ref[slot, pl.ds(rows, TILE), :].astype(F32).T[:rows, :1]
            result.append((at.astype(F32) <= info[0:1, :]) & (segs == info[1:2, :]))
        else:
            result.append(at >= seen(ref[slot, pl.ds(rows, TILE), :], info[3:4, : 2 * HD], rows))
    return result


def attend(refs, visible, norm_of, q5, rows, factor, state, seen_rows):
    keys = joined([ref[slot, pl.ds(0, rows), pl.ds(0, HD)] for ref, slot in refs])
    values = joined([ref[slot, pl.ds(0, rows), pl.ds(HD, HD)] for ref, slot in refs])
    raw = dot(keys, q5, NT)
    scores = [jnp.where(see, raw[i * rows : (i + 1) * rows], LOW) for i, see in enumerate(visible)]
    peak = jnp.max(scores[0], axis=0, keepdims=True)
    for part in scores[1:]:
        peak = jnp.maximum(peak, jnp.max(part, axis=0, keepdims=True))
    peak = peak * factor
    if seen_rows is not None:
        peak = jnp.where(seen_rows, peak, LOW)
    top, total, acc = state
    new = peak if top is None else jnp.maximum(top, peak)
    norm = new if seen_rows is None else jnp.where(seen_rows, new, HIGH)
    weights = [jnp.exp2(part * factor - norm) for part in scores]
    added = sum(jnp.sum(w, axis=0, keepdims=True) for w in weights)
    out = dot(values, joined([w.astype(BF16) for w in weights]), TN)
    if top is None:
        return new, added, out
    alpha = jnp.exp2(top - new)
    return new, total * alpha + added, acc * alpha + out


def column_refs(column, other, core):
    return [(column, 0), (column, 1), (column, 2), (other, 1), (other, 2 - 2 * core)]


def side_refs(side, other, dz):
    return [(side, dz * 2), (other, dz * 2), (side, dz * 2 + 1), (other, dz * 2 + 1)]


def pack(seg, keys, values, own, line, sem):
    rows = keys.shape[0]
    copies = [
        pltpu.make_async_copy(seg, line, sem.at[0]),
        pltpu.make_async_copy(keys, own.at[pl.ds(0, rows), pl.ds(0, HD)], sem.at[1]),
        pltpu.make_async_copy(values, own.at[pl.ds(0, rows), pl.ds(HD, HD)], sem.at[2]),
    ]
    for copy in copies:
        copy.start()
    copies[0].wait()
    own[rows:, :] = jnp.zeros((TILE, 2 * HD), BF16)
    first = lax.broadcasted_iota(jnp.int32, (TILE, rows), 0) == 0
    own[rows:, :rows] = jnp.where(first, (line[...] + 1).astype(F32), 0.0).astype(BF16)
    copies[1].wait()
    copies[2].wait()


def describe_rows(tile, rows, info):
    width = info.shape[1]
    lane = lax.broadcasted_iota(jnp.int32, (2 * HD, width), 1)
    for head in range(1, GROUP + 1):
        lane = lane - jnp.where(lane >= rows, rows, 0)
    place_in = lax.broadcasted_iota(jnp.int32, (2 * HD, width), 0)

    def picked(at):
        return dot(tile, jnp.where(place_in == at, 1.0, 0.0).astype(BF16), NN)[:1, :]

    segs, first = picked(lane), picked(0)
    info[0:1, :] = lane[:1, :].astype(F32)
    info[1:2, :] = segs
    info[2:3, :] = jnp.where(segs == first, 1.0, 0.0)
    info[3:4, :] = first
    info[4:, :] = jnp.zeros((info.shape[0] - 4, width), F32)


def forward_column(rows, factor, q, column, other, top, total, acc, q5, info):
    stack_heads(q, q5, rows)
    describe_rows(column[0, pl.ds(rows, TILE), :], rows, info)
    _, _, core = where_am_i()
    width = info.shape[1]
    near = info[2:3, :] > 0.5
    refs = column_refs(column, other, core)
    visible = masks(refs, info, rows, width, True)
    state = attend(refs[:1], visible[:1], None, q5[...], rows, factor, (None, None, None), None)
    state = attend(refs[1:], visible[1:], None, q5[...], rows, factor, state, near)
    top[...], total[...], acc[...] = state


def forward_near(
    rows, factor, weight, info, q5, partial, g2_top, g2_end, side, top, total, acc,
    top_out, total_out, acc_out, g5, held, sem,
):
    x = lax.axis_index("mp")
    part = held.shape[1]
    column = pl.multiple_of(lax.rem(x + 2, NX) * part, 128)
    copy = pltpu.make_async_copy(weight.at[:, pl.ds(column, part)], held, sem)
    copy.start()
    near = info[2:3, :] > 0.5
    state = (top[...], total[...], acc[...])
    for group in (range(0, 3), range(3, 6)):
        refs = [(side, slot) for slot in group]
        visible = masks(refs, info, rows, info.shape[1], False)
        state = attend(refs, visible, None, q5[...], rows, factor, state, near)
    top_out[...], total_out[...], acc_out[...] = state
    g2 = jnp.concatenate([g2_top[...], g2_end[...]], axis=0)
    copy.wait()
    stack_heads((partial[...] + dot(g2, held[...], NT)).astype(BF16), g5, rows)


def forward_far(
    rows, factor, weight, info, q5, g5, other, top, total, acc,
    lse, delta, here, up, down, far_top, far_end, held, attn, sem,
):
    copy = pltpu.make_async_copy(weight, held, sem)
    copy.start()
    x = lax.axis_index("mp")
    near = info[2:3, :] > 0.5
    state = (top[...], total[...], acc[...])
    for group in (range(0, 3), range(3, 6)):
        refs = [(other, slot) for slot in group]
        visible = masks(refs, info, rows, info.shape[1], False)
        state = attend(refs, visible, None, q5[...], rows, factor, state, near)
    out_t = (state[2] / state[1]).astype(BF16)
    spread_heads(out_t.T, attn, rows)
    lse[...] = state[0] + jnp.log2(state[1])
    delta[...] = jnp.sum(out_t.astype(F32) * g5[...].T.astype(F32), axis=0, keepdims=True)
    copy.wait()
    part = here.shape[1]

    def features(dx):
        column = pl.multiple_of(lax.rem(x + dx, NX) * part, 128)
        return dot(attn[...], held[:, pl.ds(column, part)], NN).astype(BF16)

    far = features(2)
    far_top[...] = far[: rows // 2]
    far_end[...] = far[rows // 2 :]
    up[...] = features(1)
    down[...] = features(3)
    here[...] = features(0)


def grads_of(refs, visible, norm, delta, q5, g5, rows, factor, scale):
    keys = joined([ref[slot, pl.ds(0, rows), pl.ds(0, HD)] for ref, slot in refs])
    values = joined([ref[slot, pl.ds(0, rows), pl.ds(HD, HD)] for ref, slot in refs])
    raw = dot(keys, q5, NT)
    slope = dot(values, g5, NT)
    weights = []
    for i, see in enumerate(visible):
        part = raw[i * rows : (i + 1) * rows] * factor - norm
        weights.append(jnp.exp2(jnp.where(see, part, LOW)))
    weights = joined(weights)
    slope = (weights * (slope - delta)).astype(BF16)
    d_value = dot(weights.astype(BF16), g5, NN).astype(BF16)
    d_key = (dot(slope, q5, NN) * scale).astype(BF16)
    return d_key, d_value, dot(keys, slope, TN)


def backward_side(rows, factor, scale, parts, info, q5, g5, lse, delta, side, other, *rest):
    if len(parts) > 1:
        column, column_other, acc, stay, leave = rest
    else:
        before, acc, stay, leave = rest
    _, _, core = where_am_i()
    width = info.shape[1]
    norm = jnp.where(info[2:3, :] > 0.5, lse[...], HIGH)
    groups = []
    for index, dz in enumerate(parts):
        outs = ((stay, 2 * index), (leave, 2 * index), (stay, 2 * index + 1), (leave, 2 * index + 1))
        groups.append((side_refs(side, other, dz - 1), outs))
    total = None
    if len(parts) > 1:
        first = 2 * len(parts)
        groups.append((column_refs(column, column_other, core)[3:], ((leave, first + 1), (leave, first + 2 - 2 * core))))
        leave[first + 2 * core] = jnp.zeros(leave.shape[1:], BF16)
    else:
        total = before[...]
    for refs, outs in groups:
        visible = masks(refs, info, rows, width, False)
        d_key, d_value, d_query = grads_of(refs, visible, norm, delta[...], q5[...], g5[...], rows, factor, scale)
        for i, (out, slot) in enumerate(outs):
            out[slot, :, :HD] = d_key[i * rows : (i + 1) * rows]
            out[slot, :, HD:] = d_value[i * rows : (i + 1) * rows]
        total = d_query if total is None else total + d_query
    acc[...] = total


def backward_column(rows, factor, scale, info, q5, g5, lse, delta, column, acc, dq, stay):
    width = info.shape[1]
    norm = jnp.where(info[2:3, :] > 0.5, lse[...], HIGH)
    refs = [(column, 0), (column, 1), (column, 2)]
    visible = masks(refs, info, rows, width, True)
    total = acc[...]
    for part, limit in ((slice(0, 1), lse[...]), (slice(1, 3), norm)):
        d_key, d_value, d_query = grads_of(
            refs[part], visible[part], limit, delta[...], q5[...], g5[...], rows, factor, scale
        )
        for i, slot in enumerate(range(3)[part]):
            stay[slot, :, :HD] = d_key[i * rows : (i + 1) * rows]
            stay[slot, :, HD:] = d_value[i * rows : (i + 1) * rows]
        total = total + d_query
    spread_heads((total * scale).astype(BF16).T, dq, rows)


def grad_heads(g0, g1, g3, weight, partial, held, weights, sem):
    x = lax.axis_index("mp")
    part = held.shape[2]
    order = (0, 1, 3)
    loads, copies = [], []
    for index, (back, piece) in enumerate(zip(order, (g0, g1, g3))):
        column = pl.multiple_of(lax.rem(x + NX - back, NX) * part, 128)
        source = weight.at[:, pl.ds(column, part)]
        loads.append(pltpu.make_async_copy(source, weights.at[index], sem.at[2 * index]))
        copies.append(pltpu.make_async_copy(piece, held.at[index], sem.at[2 * index + 1]))
        loads[-1].start()
        copies[-1].start()
    total = None
    for index in range(len(order)):
        loads[index].wait()
        copies[index].wait()
        term = dot(held[index], weights[index], NT)
        total = term if total is None else total + term
    partial[...] = total


def join_features(here, up, down, out):
    out[...] = (here[...].astype(F32) + up[...].astype(F32) + down[...].astype(F32)).astype(BF16)


def add_up(*terms):
    return sum(t.astype(F32) for t in terms)


def per_device(queries, keys, values, seg_ids, out_weight, grad_out):
    rows = queries.shape[0]
    scale = 1.0 / math.sqrt(HD)
    factor = scale * math.log2(math.e)
    width = -(-GROUP * rows // 128) * 128
    y, z, _ = where_am_i()
    x = lax.axis_index("mp")
    vmem = pl.BlockSpec(memory_space=pltpu.VMEM)

    def shape(*dims, dtype=BF16):
        return jax.ShapeDtypeStruct(dims, dtype)

    anywhere = pl.BlockSpec(memory_space=pl.ANY)

    fixed = pl.BlockSpec(memory_space=pltpu.HBM)

    def call(body, outs, micros, *operands, loose=0, pinned=0, scratch=(), mib=24):
        return pl.pallas_call(
            body,
            out_shape=outs,
            in_specs=[anywhere] * loose
            + [fixed] * pinned
            + [vmem] * (len(operands) - loose - pinned),
            out_specs=jax.tree.map(lambda _: vmem, outs),
            scratch_shapes=scratch,
            cost_estimate=pl.CostEstimate(flops=micros * 1_153_000_000, bytes_accessed=0, transcendentals=0),
            compiler_params=pltpu.CompilerParams(vmem_limit_bytes=mib * 1024 * 1024),
        )(*operands)

    line = shape(1, width, dtype=F32)
    square = shape(HD, width, dtype=F32)
    stacked = shape(width, HD)
    half = rows // 2

    own = call(
        pack, shape(rows + TILE, 2 * HD), 1, seg_ids.reshape(1, rows), keys, values, pinned=3, mib=60,
        scratch=[pltpu.VMEM((1, rows), jnp.int32), pltpu.SemaphoreType.DMA((3,))],
    )
    own, grad_out = lax.optimization_barrier((own, grad_out))
    y1, y2 = move(own, dy=1), move(own, dy=2)
    g1, g3 = move_x(grad_out, 1), move_x(grad_out, 3)
    y1, y2 = lax.optimization_barrier((y1, y2))
    y1, y2 = jnp.where(y >= 1, y1, 0), jnp.where(y >= 2, y2, 0)

    column = jnp.stack([own, y1, y2])
    column_other = move(column, flip=1)
    sides = {dz: jnp.stack([y1, jnp.where(z + dz < NZ, own, y2)]) for dz in (2, 1, 3)}
    sides[3], column_other = lax.optimization_barrier((sides[3], column_other))
    sides = [move(sides[dz], dz=dz) for dz in (1, 2, 3)]
    g2_top, g2_end = move_x(g1[:half], 1), move_x(g3[half:], 3)
    top, total, acc, q5, info = call(
        lambda *refs: forward_column(rows, factor, *refs),
        (line, line, square, stacked, shape(8, width, dtype=F32)), 1, queries, column, column_other,
    )
    part = grad_out.shape[1]
    partial = call(
        grad_heads, shape(rows, GROUP * HD, dtype=F32), 3, grad_out, g1, g3, out_weight, loose=3, pinned=1,
        scratch=[
            pltpu.VMEM((NX - 1, rows, part), BF16),
            pltpu.VMEM((NX - 1, out_weight.shape[0], part), BF16),
            pltpu.SemaphoreType.DMA((2 * (NX - 1),)),
        ],
    )
    *sides, g2_top, g2_end, top, partial = lax.optimization_barrier((*sides, g2_top, g2_end, top, partial))

    side = jnp.concatenate(sides)
    side_other = move(side, flip=1)
    top, total, acc, g5, side_other = lax.optimization_barrier(
        (
            *call(
                lambda *refs: forward_near(rows, factor, *refs),
                (line, line, square, stacked), 4,
                out_weight, info, q5, partial, g2_top, g2_end, side, top, total, acc, pinned=1,
                scratch=[pltpu.VMEM((out_weight.shape[0], part), BF16), pltpu.SemaphoreType.DMA],
            ),
            side_other,
        )
    )
    whole, halved = shape(rows, part), shape(half, part)
    lse, delta, here, up, down, *far = call(
        lambda *refs: forward_far(rows, factor, *refs),
        (line, line, whole, whole, whole, halved, halved), 6,
        out_weight, info, q5, g5, side_other, top, total, acc, pinned=1, mib=30,
        scratch=[
            pltpu.VMEM(out_weight.shape, BF16),
            pltpu.VMEM((rows, GROUP * HD), BF16),
            pltpu.SemaphoreType.DMA,
        ],
    )
    early = (move_x(far[0], 1), move_x(far[1], 3))

    def side_grads(parts, kept, sent, micros, *more):
        return call(
            lambda *refs: backward_side(rows, factor, scale, parts, *refs),
            (square, shape(kept, rows, 2 * HD), shape(sent, rows, 2 * HD)), micros,
            info, q5, g5, lse, delta, side, side_other, *more,
        )

    acc, stay, leave, *early = lax.optimization_barrier(
        (*side_grads((2, 1), 4, 7, 7, column, column_other), *early)
    )
    up = jnp.concatenate([add_up(up[:half], early[0]).astype(BF16), up[half:]], axis=0)
    down = jnp.concatenate([down[:half], add_up(down[half:], early[1]).astype(BF16)], axis=0)
    other = move(leave, flip=1)
    acc, stay_last, leave_last, other = lax.optimization_barrier((*side_grads((3,), 2, 2, 3, acc), other))
    other_last = move(leave_last, flip=1)
    mixed = add_up(stay, other[:4]).astype(BF16)
    returned = {2: move(mixed[:2], dz=-2), 1: move(mixed[2:], dz=-1)}
    returned[3] = move(add_up(stay_last, other_last).astype(BF16), dz=-3)
    up, down = move_x(up, 1), move_x(down, 3)
    grad_query, stay, returned[1], returned[2], returned[3], up, down = lax.optimization_barrier(
        (
            *call(
                lambda *refs: backward_column(rows, factor, scale, *refs),
                (shape(rows, GROUP * HD), shape(3, rows, 2 * HD)), 3,
                info, q5, g5, lse, delta, column, acc,
            ),
            returned[1], returned[2], returned[3], up, down,
        )
    )
    projected = add_up(here, up, down).astype(BF16)
    mixed = add_up(stay, other[4:])
    first, second, third = mixed[0], mixed[1], mixed[2]
    for dz in range(1, NZ):
        far, near = returned[dz][0].astype(F32), returned[dz][1].astype(F32)
        second = second + far
        first = first + jnp.where(z + dz < NZ, near, 0.0)
        third = third + jnp.where(z + dz < NZ, 0.0, near)
    second, third = second.astype(BF16), third.astype(BF16)
    grads = add_up(first, move(second, dy=-1), move(third, dy=-2)).astype(BF16)
    return (projected, grad_query, grads[:, :HD], grads[:, HD:])


def solution(mesh):
    return jax.shard_map(
        per_device,
        mesh=mesh,
        in_specs=(
            P("dp", "mp"),
            P("dp", "mp"),
            P("dp", "mp"),
            P("dp"),
            P("mp", None),
            P("dp", "mp"),
        ),
        out_specs=(P("dp", "mp"), P("dp", "mp"), P("dp", "mp"), P("dp", "mp")),
        check_vma=False,
    )
```

```python
import math

import jax
import jax.numpy as jnp
from jax import lax
from jax.experimental import pallas as pl
from jax.experimental.pallas import tpu as pltpu
from jax.sharding import PartitionSpec as P

HD = 128
GROUP = 5
NX = 4
NY = 4
NZ = 4
TILE = 16
LOW = -1e30
HIGH = 1e30
F32 = jnp.float32
BF16 = jnp.bfloat16
NT = (((1,), (1,)), ((), ()))
TN = (((0,), (0,)), ((), ()))
NN = (((1,), (0,)), ((), ()))


def place(y, z, core):
    return ((y % NY) * NZ + (z % NZ)) * 2 + core


def shift(dy, dz, flip):
    pairs = []
    for y in range(NY):
        for z in range(NZ):
            for core in range(2):
                pairs.append((place(y, z, core), place(y + dy, z + dz, core ^ flip)))
    return pairs


def move(value, dy=0, dz=0, flip=0):
    return lax.ppermute(value, "dp", shift(dy, dz, flip))


def move_x(value, dx):
    return lax.ppermute(value, "mp", [(x, (x + dx) % NX) for x in range(NX)])


def dot(a, b, dims):
    return lax.dot_general(a, b, dims, preferred_element_type=F32)


def where_am_i():
    index = lax.axis_index("dp")
    return index // (2 * NZ), (index // 2) % NZ, index % 2


def stack_heads(source, target, rows):
    for head in range(GROUP):
        target[head * rows : (head + 1) * rows, :] = source[:, head * HD : (head + 1) * HD]
    target[GROUP * rows :, :] = jnp.zeros((target.shape[0] - GROUP * rows, HD), BF16)


def spread_heads(stacked, target, rows):
    for head in range(GROUP):
        target[:, head * HD : (head + 1) * HD] = stacked[head * rows : (head + 1) * rows, :]


def joined(parts):
    return parts[0] if len(parts) == 1 else jnp.concatenate(parts, axis=0)


def seen(tile, seg, rows):
    match = jnp.sum(jnp.where(tile.astype(F32) == seg, 1.0, 0.0), axis=0, keepdims=True)
    return rows - jnp.sum(match, axis=1, keepdims=True)


def masks(refs, info, rows, width, own):
    at = lax.broadcasted_iota(jnp.int32, (rows, width), 0).astype(F32)
    result = []
    for index, (ref, slot) in enumerate(refs):
        if own and index == 0:
            segs = ref[slot, pl.ds(rows, TILE), :].astype(F32).T[:rows, :1]
            result.append((at <= info[0:1, :]) & (segs == info[1:2, :]))
        else:
            result.append(at >= seen(ref[slot, pl.ds(rows, TILE), :], info[3:4, : 2 * HD], rows))
    return result


def attend(refs, visible, norm_of, q5, rows, factor, state, seen_rows):
    keys = joined([ref[slot, pl.ds(0, rows), pl.ds(0, HD)] for ref, slot in refs])
    values = joined([ref[slot, pl.ds(0, rows), pl.ds(HD, HD)] for ref, slot in refs])
    raw = dot(keys, q5, NT)
    scores = [jnp.where(see, raw[i * rows : (i + 1) * rows], LOW) for i, see in enumerate(visible)]
    peak = jnp.max(scores[0], axis=0, keepdims=True)
    for part in scores[1:]:
        peak = jnp.maximum(peak, jnp.max(part, axis=0, keepdims=True))
    peak = peak * factor
    if seen_rows is not None:
        peak = jnp.where(seen_rows, peak, LOW)
    top, total, acc = state
    new = peak if top is None else jnp.maximum(top, peak)
    norm = new if seen_rows is None else jnp.where(seen_rows, new, HIGH)
    weights = [jnp.exp2(part * factor - norm) for part in scores]
    added = sum(jnp.sum(w, axis=0, keepdims=True) for w in weights)
    out = dot(values, joined([w.astype(BF16) for w in weights]), TN)
    if top is None:
        return new, added, out
    alpha = jnp.exp2(top - new)
    return new, total * alpha + added, acc * alpha + out


def column_refs(column):
    return [(column, 0), (column, 1), (column, 2)]


def beside_refs(other, core):
    return [(other, 2 * NZ - 1), (other, 2 * NZ - 2 * core)]


def side_refs(side, other, dz):
    return [(side, dz * 2), (other, dz * 2), (side, dz * 2 + 1), (other, dz * 2 + 1)]


def pack(seg, keys, values, own, line, sem):
    rows = keys.shape[0]
    copies = [
        pltpu.make_async_copy(seg, line, sem.at[0]),
        pltpu.make_async_copy(keys, own.at[pl.ds(0, rows), pl.ds(0, HD)], sem.at[1]),
        pltpu.make_async_copy(values, own.at[pl.ds(0, rows), pl.ds(HD, HD)], sem.at[2]),
    ]
    for copy in copies:
        copy.start()
    copies[0].wait()
    own[rows:, :] = jnp.zeros((TILE, 2 * HD), BF16)
    first = lax.broadcasted_iota(jnp.int32, (TILE, rows), 0) == 0
    own[rows:, :rows] = jnp.where(first, (line[...] + 1).astype(F32), 0.0).astype(BF16)
    copies[1].wait()
    copies[2].wait()


def describe_rows(tile, rows, info):
    width = info.shape[1]
    lane = lax.broadcasted_iota(jnp.int32, (2 * HD, width), 1)
    for head in range(1, GROUP + 1):
        lane = lane - jnp.where(lane >= rows, rows, 0)
    place_in = lax.broadcasted_iota(jnp.int32, (2 * HD, width), 0)

    def picked(at):
        return dot(tile, jnp.where(place_in == at, 1.0, 0.0).astype(BF16), NN)[:1, :]

    segs, first = picked(lane), picked(0)
    info[0:1, :] = lane[:1, :].astype(F32)
    info[1:2, :] = segs
    info[2:3, :] = jnp.where(segs == first, 1.0, 0.0)
    info[3:4, :] = first
    info[4:, :] = jnp.zeros((info.shape[0] - 4, width), F32)


def forward_column(rows, factor, q, column, top, total, acc, q5, info):
    stack_heads(q, q5, rows)
    describe_rows(column[0, pl.ds(rows, TILE), :], rows, info)
    width = info.shape[1]
    near = info[2:3, :] > 0.5
    refs = column_refs(column)
    visible = masks(refs, info, rows, width, True)
    state = attend(refs[:1], visible[:1], None, q5[...], rows, factor, (None, None, None), None)
    state = attend(refs[1:], visible[1:], None, q5[...], rows, factor, state, near)
    top[...], total[...], acc[...] = state


def forward_near(rows, factor, info, q5, side, top, total, acc, top_out, total_out, acc_out):
    near = info[2:3, :] > 0.5
    state = (top[...], total[...], acc[...])
    for group in (range(0, 3), range(3, 6)):
        refs = [(side, slot) for slot in group]
        visible = masks(refs, info, rows, info.shape[1], False)
        state = attend(refs, visible, None, q5[...], rows, factor, state, near)
    top_out[...], total_out[...], acc_out[...] = state


def forward_far(
    rows, factor, weight, info, q5, other, top, total, acc,
    lse, attn_t, here, up, down, far_top, far_end, held, attn, sem,
):
    copy = pltpu.make_async_copy(weight, held, sem)
    copy.start()
    x = lax.axis_index("mp")
    _, _, core = where_am_i()
    near = info[2:3, :] > 0.5
    state = (top[...], total[...], acc[...])
    shards = [(other, slot) for slot in range(2 * NZ - 2)] + beside_refs(other, core)
    for refs in (shards[:4], shards[4:]):
        visible = masks(refs, info, rows, info.shape[1], False)
        state = attend(refs, visible, None, q5[...], rows, factor, state, near)
    out_t = (state[2] / state[1]).astype(BF16)
    spread_heads(out_t.T, attn, rows)
    lse[...] = state[0] + jnp.log2(state[1])
    attn_t[...] = out_t
    copy.wait()
    part = here.shape[1]

    def features(dx):
        column = pl.multiple_of(lax.rem(x + dx, NX) * part, 128)
        return dot(attn[...], held[:, pl.ds(column, part)], NN).astype(BF16)

    far = features(2)
    far_top[...] = far[: rows // 2]
    far_end[...] = far[rows // 2 :]
    up[...] = features(1)
    down[...] = features(3)
    here[...] = features(0)


def grads_of(refs, visible, norm, delta, q5, g5, rows, factor, scale):
    keys = joined([ref[slot, pl.ds(0, rows), pl.ds(0, HD)] for ref, slot in refs])
    values = joined([ref[slot, pl.ds(0, rows), pl.ds(HD, HD)] for ref, slot in refs])
    raw = dot(keys, q5, NT)
    slope = dot(values, g5, NT)
    weights = []
    for i, see in enumerate(visible):
        part = raw[i * rows : (i + 1) * rows] * factor - norm
        weights.append(jnp.exp2(jnp.where(see, part, LOW)))
    weights = joined(weights)
    slope = (weights * (slope - delta)).astype(BF16)
    d_value = dot(weights.astype(BF16), g5, NN).astype(BF16)
    d_key = (dot(slope, q5, NN) * scale).astype(BF16)
    return d_key, d_value, dot(keys, slope, TN)


def backward_parts(rows, factor, scale, groups, info, q5, g5, lse, delta, total, acc):
    norm = jnp.where(info[2:3, :] > 0.5, lse[...], HIGH)
    for refs, outs in groups:
        visible = masks(refs, info, rows, info.shape[1], False)
        d_key, d_value, d_query = grads_of(refs, visible, norm, delta[...], q5[...], g5[...], rows, factor, scale)
        for i, (out, slot) in enumerate(outs):
            out[slot, :, :HD] = d_key[i * rows : (i + 1) * rows]
            out[slot, :, HD:] = d_value[i * rows : (i + 1) * rows]
        total = d_query if total is None else total + d_query
    acc[...] = total


def side_group(side, other, dz, stay, leave, at):
    return side_refs(side, other, dz - 1), ((stay, at), (leave, at), (stay, at + 1), (leave, at + 1))


def backward_first(
    rows, factor, scale, weight, info, q5, partial, g2_top, g2_end, attn_t, lse, side, other,
    acc, stay, leave, g5, delta, held, sem,
):
    x = lax.axis_index("mp")
    column = pl.multiple_of(lax.rem(x + 2, NX) * held.shape[1], 128)
    copy = pltpu.make_async_copy(weight.at[:, pl.ds(column, held.shape[1])], held, sem)
    copy.start()
    _, _, core = where_am_i()
    leave[4 + 2 * core] = jnp.zeros(leave.shape[1:], BF16)
    g2 = jnp.concatenate([g2_top[...], g2_end[...]], axis=0)
    copy.wait()
    stack_heads((partial[...] + dot(g2, held[...], NT)).astype(BF16), g5, rows)
    delta[...] = jnp.sum(attn_t[...].astype(F32) * g5[...].T.astype(F32), axis=0, keepdims=True)
    groups = [
        side_group(side, other, 2, stay, leave, 0),
        side_group(side, other, 1, stay, leave, 2),
        (beside_refs(other, core), ((leave, 5), (leave, 6 - 2 * core))),
    ]
    backward_parts(rows, factor, scale, groups, info, q5, g5, lse, delta, None, acc)


def backward_second(rows, factor, scale, info, q5, g5, lse, delta, side, other, before, acc, stay, leave):
    groups = [side_group(side, other, 3, stay, leave, 0)]
    backward_parts(rows, factor, scale, groups, info, q5, g5, lse, delta, before[...], acc)


def backward_column(rows, factor, scale, info, q5, g5, lse, delta, column, acc, dq, stay):
    width = info.shape[1]
    norm = jnp.where(info[2:3, :] > 0.5, lse[...], HIGH)
    refs = column_refs(column)
    visible = masks(refs, info, rows, width, True)
    total = acc[...]
    for part, limit in ((slice(0, 1), lse[...]), (slice(1, 3), norm)):
        d_key, d_value, d_query = grads_of(
            refs[part], visible[part], limit, delta[...], q5[...], g5[...], rows, factor, scale
        )
        for i, slot in enumerate(range(3)[part]):
            stay[slot, :, :HD] = d_key[i * rows : (i + 1) * rows]
            stay[slot, :, HD:] = d_value[i * rows : (i + 1) * rows]
        total = total + d_query
    spread_heads((total * scale).astype(BF16).T, dq, rows)


def grad_heads(g0, g1, g3, weight, partial, held, weights, sem):
    x = lax.axis_index("mp")
    part = held.shape[2]
    order = (0, 1, 3)
    loads, copies = [], []
    for index, (back, piece) in enumerate(zip(order, (g0, g1, g3))):
        column = pl.multiple_of(lax.rem(x + NX - back, NX) * part, 128)
        source = weight.at[:, pl.ds(column, part)]
        loads.append(pltpu.make_async_copy(source, weights.at[index], sem.at[2 * index]))
        copies.append(pltpu.make_async_copy(piece, held.at[index], sem.at[2 * index + 1]))
        loads[-1].start()
        copies[-1].start()
    total = None
    for index in range(len(order)):
        loads[index].wait()
        copies[index].wait()
        term = dot(held[index], weights[index], NT)
        total = term if total is None else total + term
    partial[...] = total


def join_features(here, up, down, out):
    out[...] = (here[...].astype(F32) + up[...].astype(F32) + down[...].astype(F32)).astype(BF16)


def add_up(*terms):
    return sum(t.astype(F32) for t in terms)


def per_device(queries, keys, values, seg_ids, out_weight, grad_out):
    rows = queries.shape[0]
    scale = 1.0 / math.sqrt(HD)
    factor = scale * math.log2(math.e)
    width = -(-GROUP * rows // 128) * 128
    y, z, _ = where_am_i()
    x = lax.axis_index("mp")
    vmem = pl.BlockSpec(memory_space=pltpu.VMEM)

    def shape(*dims, dtype=BF16):
        return jax.ShapeDtypeStruct(dims, dtype)

    anywhere = pl.BlockSpec(memory_space=pl.ANY)

    fixed = pl.BlockSpec(memory_space=pltpu.HBM)

    def call(body, outs, micros, *operands, loose=0, pinned=0, scratch=(), mib=24):
        return pl.pallas_call(
            body,
            out_shape=outs,
            in_specs=[anywhere] * loose
            + [fixed] * pinned
            + [vmem] * (len(operands) - loose - pinned),
            out_specs=jax.tree.map(lambda _: vmem, outs),
            scratch_shapes=scratch,
            cost_estimate=pl.CostEstimate(flops=micros * 1_153_000_000, bytes_accessed=0, transcendentals=0),
            compiler_params=pltpu.CompilerParams(vmem_limit_bytes=mib * 1024 * 1024),
        )(*operands)

    line = shape(1, width, dtype=F32)
    square = shape(HD, width, dtype=F32)
    stacked = shape(width, HD)
    half = rows // 2

    own = call(
        pack, shape(rows + TILE, 2 * HD), 1, seg_ids.reshape(1, rows), keys, values, pinned=3, mib=60,
        scratch=[pltpu.VMEM((1, rows), jnp.int32), pltpu.SemaphoreType.DMA((3,))],
    )
    y1, y2 = move(own, dy=1), move(own, dy=2)
    g1, g3 = move_x(grad_out, 1), move_x(grad_out, 3)
    y1, y2 = lax.optimization_barrier((y1, y2))
    y1, y2 = jnp.where(y >= 1, y1, 0), jnp.where(y >= 2, y2, 0)

    column = jnp.stack([own, y1, y2])
    sides = {dz: jnp.stack([y1, jnp.where(z + dz < NZ, own, y2)]) for dz in (2, 1, 3)}
    sides = [move(sides[dz], dz=dz) for dz in (1, 2, 3)]
    g2_top, g2_end = move_x(g1[:half], 1), move_x(g3[half:], 3)
    top, total, acc, q5, info = call(
        lambda *refs: forward_column(rows, factor, *refs),
        (line, line, square, stacked, shape(8, width, dtype=F32)), 1, queries, column,
    )
    part = grad_out.shape[1]
    partial = call(
        grad_heads, shape(rows, GROUP * HD, dtype=F32), 3, grad_out, g1, g3, out_weight, loose=3, pinned=1,
        scratch=[
            pltpu.VMEM((NX - 1, rows, part), BF16),
            pltpu.VMEM((NX - 1, out_weight.shape[0], part), BF16),
            pltpu.SemaphoreType.DMA((2 * (NX - 1),)),
        ],
    )
    *sides, top, partial = lax.optimization_barrier((*sides, top, partial))

    side = jnp.concatenate([*sides, column])
    side_other = move(side, flip=1)
    top, total, acc, side_other = lax.optimization_barrier(
        (
            *call(
                lambda *refs: forward_near(rows, factor, *refs),
                (line, line, square), 4, info, q5, side, top, total, acc,
            ),
            side_other,
        )
    )
    whole, halved = shape(rows, part), shape(half, part)
    lse, attn_t, here, up, down, *far = call(
        lambda *refs: forward_far(rows, factor, *refs),
        (line, shape(HD, width), whole, whole, whole, halved, halved), 1,
        out_weight, info, q5, side_other, top, total, acc, pinned=1, mib=30,
        scratch=[
            pltpu.VMEM(out_weight.shape, BF16),
            pltpu.VMEM((rows, GROUP * HD), BF16),
            pltpu.SemaphoreType.DMA,
        ],
    )
    lse, *far, g2_top, g2_end = lax.optimization_barrier((lse, *far, g2_top, g2_end))
    early = (move_x(far[0], 1), move_x(far[1], 3))

    def pieces(count):
        return shape(count, rows, 2 * HD)

    acc, stay, leave, g5, delta, *early = lax.optimization_barrier(
        (
            *call(
                lambda *refs: backward_first(rows, factor, scale, *refs),
                (square, pieces(4), pieces(7), stacked, line), 8,
                out_weight, info, q5, partial, g2_top, g2_end, attn_t, lse, side, side_other, pinned=1,
                scratch=[pltpu.VMEM((out_weight.shape[0], part), BF16), pltpu.SemaphoreType.DMA],
            ),
            *early,
        )
    )
    up = jnp.concatenate([add_up(up[:half], early[0]).astype(BF16), up[half:]], axis=0)
    down = jnp.concatenate([down[:half], add_up(down[half:], early[1]).astype(BF16)], axis=0)
    other = move(leave, flip=1)
    acc, stay_last, leave_last, other = lax.optimization_barrier(
        (
            *call(
                lambda *refs: backward_second(rows, factor, scale, *refs),
                (square, pieces(2), pieces(2)), 3, info, q5, g5, lse, delta, side, side_other, acc,
            ),
            other,
        )
    )
    other_last = move(leave_last, flip=1)
    mixed = add_up(stay, other[:4]).astype(BF16)
    returned = {2: move(mixed[:2], dz=-2), 1: move(mixed[2:], dz=-1)}
    returned[3] = move(add_up(stay_last, other_last).astype(BF16), dz=-3)
    up, down = move_x(up, 1), move_x(down, 3)
    grad_query, stay, returned[1], returned[2], returned[3], up, down = lax.optimization_barrier(
        (
            *call(
                lambda *refs: backward_column(rows, factor, scale, *refs),
                (shape(rows, GROUP * HD), pieces(3)), 3,
                info, q5, g5, lse, delta, column, acc,
            ),
            returned[1], returned[2], returned[3], up, down,
        )
    )
    projected = add_up(here, up, down).astype(BF16)
    mixed = add_up(stay, other[4:])
    first, second, third = mixed[0], mixed[1], mixed[2]
    for dz in range(1, NZ):
        far, near = returned[dz][0].astype(F32), returned[dz][1].astype(F32)
        second = second + far
        first = first + jnp.where(z + dz < NZ, near, 0.0)
        third = third + jnp.where(z + dz < NZ, 0.0, near)
    second, third = second.astype(BF16), third.astype(BF16)
    grads = add_up(first, move(second, dy=-1), move(third, dy=-2)).astype(BF16)
    return (projected, grad_query, grads[:, :HD], grads[:, HD:])


def solution(mesh):
    return jax.shard_map(
        per_device,
        mesh=mesh,
        in_specs=(
            P("dp", "mp"),
            P("dp", "mp"),
            P("dp", "mp"),
            P("dp"),
            P("mp", None),
            P("dp", "mp"),
        ),
        out_specs=(P("dp", "mp"), P("dp", "mp"), P("dp", "mp"), P("dp", "mp")),
        check_vma=False,
    )
```

```python
import math

import jax
import jax.numpy as jnp
from jax import lax
from jax.experimental import pallas as pl
from jax.experimental.pallas import tpu as pltpu
from jax.sharding import PartitionSpec as P

HD = 128
GROUP = 5
NX = 4
NY = 4
NZ = 4
TILE = 16
LOW = -1e30
HIGH = 1e30
F32 = jnp.float32
BF16 = jnp.bfloat16
NT = (((1,), (1,)), ((), ()))
TN = (((0,), (0,)), ((), ()))
NN = (((1,), (0,)), ((), ()))


def place(y, z, core):
    return ((y % NY) * NZ + (z % NZ)) * 2 + core


def shift(dy, dz, flip):
    pairs = []
    for y in range(NY):
        for z in range(NZ):
            for core in range(2):
                pairs.append((place(y, z, core), place(y + dy, z + dz, core ^ flip)))
    return pairs


def move(value, dy=0, dz=0, flip=0):
    return lax.ppermute(value, "dp", shift(dy, dz, flip))


def move_x(value, dx):
    return lax.ppermute(value, "mp", [(x, (x + dx) % NX) for x in range(NX)])


def dot(a, b, dims):
    return lax.dot_general(a, b, dims, preferred_element_type=F32)


def where_am_i():
    index = lax.axis_index("dp")
    return index // (2 * NZ), (index // 2) % NZ, index % 2


def stack_heads(source, target, rows):
    for head in range(GROUP):
        target[head * rows : (head + 1) * rows, :] = source[:, head * HD : (head + 1) * HD]
    target[GROUP * rows :, :] = jnp.zeros((target.shape[0] - GROUP * rows, HD), BF16)


def spread_heads(stacked, target, rows):
    for head in range(GROUP):
        target[:, head * HD : (head + 1) * HD] = stacked[head * rows : (head + 1) * rows, :]


def joined(parts):
    return parts[0] if len(parts) == 1 else jnp.concatenate(parts, axis=0)


def seen(tile, seg, rows):
    match = jnp.sum(jnp.where(tile.astype(F32) == seg, 1.0, 0.0), axis=0, keepdims=True)
    return rows - jnp.sum(match, axis=1, keepdims=True)


def masks(refs, info, rows, width, own):
    at = lax.broadcasted_iota(jnp.int32, (rows, width), 0).astype(F32)
    result = []
    for index, (ref, slot) in enumerate(refs):
        if own and index == 0:
            segs = ref[slot, pl.ds(rows, TILE), :].astype(F32).T[:rows, :1]
            result.append((at <= info[0:1, :]) & (segs == info[1:2, :]))
        else:
            result.append(at >= seen(ref[slot, pl.ds(rows, TILE), :], info[3:4, : 2 * HD], rows))
    return result


def attend(refs, visible, norm_of, q5, rows, factor, state, seen_rows):
    keys = joined([ref[slot, pl.ds(0, rows), pl.ds(0, HD)] for ref, slot in refs])
    values = joined([ref[slot, pl.ds(0, rows), pl.ds(HD, HD)] for ref, slot in refs])
    raw = dot(keys, q5, NT)
    scores = [jnp.where(see, raw[i * rows : (i + 1) * rows], LOW) for i, see in enumerate(visible)]
    peak = jnp.max(scores[0], axis=0, keepdims=True)
    for part in scores[1:]:
        peak = jnp.maximum(peak, jnp.max(part, axis=0, keepdims=True))
    peak = peak * factor
    if seen_rows is not None:
        peak = jnp.where(seen_rows, peak, LOW)
    top, total, acc = state
    new = peak if top is None else jnp.maximum(top, peak)
    norm = new if seen_rows is None else jnp.where(seen_rows, new, HIGH)
    weights = [jnp.exp2(part * factor - norm) for part in scores]
    added = sum(jnp.sum(w, axis=0, keepdims=True) for w in weights)
    out = dot(values, joined([w.astype(BF16) for w in weights]), TN)
    if top is None:
        return new, added, out
    alpha = jnp.exp2(top - new)
    return new, total * alpha + added, acc * alpha + out


def column_refs(column):
    return [(column, 0), (column, 1), (column, 2)]


def beside_refs(other, core):
    return [(other, 2 * NZ - 1), (other, 2 * NZ - 2 * core)]


def side_refs(side, other, dz):
    return [(side, dz * 2), (other, dz * 2), (side, dz * 2 + 1), (other, dz * 2 + 1)]


def pack(seg, keys, values, own, line, sem):
    rows = keys.shape[0]
    copies = [
        pltpu.make_async_copy(seg, line, sem.at[0]),
        pltpu.make_async_copy(keys, own.at[pl.ds(0, rows), pl.ds(0, HD)], sem.at[1]),
        pltpu.make_async_copy(values, own.at[pl.ds(0, rows), pl.ds(HD, HD)], sem.at[2]),
    ]
    for copy in copies:
        copy.start()
    copies[0].wait()
    own[rows:, :] = jnp.zeros((TILE, 2 * HD), BF16)
    first = lax.broadcasted_iota(jnp.int32, (TILE, rows), 0) == 0
    own[rows:, :rows] = jnp.where(first, (line[...] + 1).astype(F32), 0.0).astype(BF16)
    copies[1].wait()
    copies[2].wait()


def describe_rows(tile, rows, info):
    width = info.shape[1]
    lane = lax.broadcasted_iota(jnp.int32, (2 * HD, width), 1)
    for head in range(1, GROUP + 1):
        lane = lane - jnp.where(lane >= rows, rows, 0)
    place_in = lax.broadcasted_iota(jnp.int32, (2 * HD, width), 0)

    def picked(at):
        return dot(tile, jnp.where(place_in == at, 1.0, 0.0).astype(BF16), NN)[:1, :]

    segs, first = picked(lane), picked(0)
    info[0:1, :] = lane[:1, :].astype(F32)
    info[1:2, :] = segs
    info[2:3, :] = jnp.where(segs == first, 1.0, 0.0)
    info[3:4, :] = first
    info[4:, :] = jnp.zeros((info.shape[0] - 4, width), F32)


def forward_column(rows, factor, q, column, top, total, acc, q5, info):
    stack_heads(q, q5, rows)
    describe_rows(column[0, pl.ds(rows, TILE), :], rows, info)
    width = info.shape[1]
    near = info[2:3, :] > 0.5
    refs = column_refs(column)
    visible = masks(refs, info, rows, width, True)
    state = attend(refs[:1], visible[:1], None, q5[...], rows, factor, (None, None, None), None)
    state = attend(refs[1:], visible[1:], None, q5[...], rows, factor, state, near)
    top[...], total[...], acc[...] = state


def forward_near(rows, factor, info, q5, side, top, total, acc, top_out, total_out, acc_out):
    near = info[2:3, :] > 0.5
    state = (top[...], total[...], acc[...])
    for group in (range(0, 3), range(3, 6)):
        refs = [(side, slot) for slot in group]
        visible = masks(refs, info, rows, info.shape[1], False)
        state = attend(refs, visible, None, q5[...], rows, factor, state, near)
    top_out[...], total_out[...], acc_out[...] = state


def forward_far(
    rows, factor, weight, info, q5, other, top, total, acc,
    lse, attn_t, attn, up, down, far_top, far_end, held, sem,
):
    copy = pltpu.make_async_copy(weight, held, sem)
    copy.start()
    x = lax.axis_index("mp")
    _, _, core = where_am_i()
    near = info[2:3, :] > 0.5
    state = (top[...], total[...], acc[...])
    shards = [(other, slot) for slot in range(2 * NZ - 2)] + beside_refs(other, core)
    for refs in (shards,):
        visible = masks(refs, info, rows, info.shape[1], False)
        state = attend(refs, visible, None, q5[...], rows, factor, state, near)
    out_t = (state[2] / state[1]).astype(BF16)
    spread_heads(out_t.T, attn, rows)
    lse[...] = state[0] + jnp.log2(state[1])
    attn_t[...] = out_t
    copy.wait()
    part = up.shape[1]

    def features(dx):
        column = pl.multiple_of(lax.rem(x + dx, NX) * part, 128)
        return dot(attn[...], held[:, pl.ds(column, part)], NN).astype(BF16)

    far = features(2)
    far_top[...] = far[: rows // 2]
    far_end[...] = far[rows // 2 :]
    up[...] = features(1)
    down[...] = features(3)


def grads_of(refs, visible, norm, delta, q5, g5, rows, factor, scale):
    keys = joined([ref[slot, pl.ds(0, rows), pl.ds(0, HD)] for ref, slot in refs])
    values = joined([ref[slot, pl.ds(0, rows), pl.ds(HD, HD)] for ref, slot in refs])
    raw = dot(keys, q5, NT)
    slope = dot(values, g5, NT)
    weights = []
    for i, see in enumerate(visible):
        part = raw[i * rows : (i + 1) * rows] * factor - norm
        weights.append(jnp.exp2(jnp.where(see, part, LOW)))
    weights = joined(weights)
    slope = (weights * (slope - delta)).astype(BF16)
    d_value = dot(weights.astype(BF16), g5, NN).astype(BF16)
    d_key = (dot(slope, q5, NN) * scale).astype(BF16)
    return d_key, d_value, dot(keys, slope, TN)


def backward_parts(rows, factor, scale, groups, info, q5, g5, lse, delta, total, acc):
    norm = jnp.where(info[2:3, :] > 0.5, lse[...], HIGH)
    for refs, outs in groups:
        visible = masks(refs, info, rows, info.shape[1], False)
        d_key, d_value, d_query = grads_of(refs, visible, norm, delta[...], q5[...], g5[...], rows, factor, scale)
        for i, (out, slot) in enumerate(outs):
            out[slot, :, :HD] = d_key[i * rows : (i + 1) * rows]
            out[slot, :, HD:] = d_value[i * rows : (i + 1) * rows]
        total = d_query if total is None else total + d_query
    acc[...] = total


def side_group(side, other, dz, stay, leave, at):
    return side_refs(side, other, dz - 1), ((stay, at), (leave, at), (stay, at + 1), (leave, at + 1))


def backward_first(
    rows, factor, scale, weight, info, q5, partial, g2_top, g2_end, attn_t, lse, side, other,
    acc, stay, leave, g5, delta, held, sem,
):
    x = lax.axis_index("mp")
    column = pl.multiple_of(lax.rem(x + 2, NX) * held.shape[1], 128)
    copy = pltpu.make_async_copy(weight.at[:, pl.ds(column, held.shape[1])], held, sem)
    copy.start()
    _, _, core = where_am_i()
    leave[4 + 2 * core] = jnp.zeros(leave.shape[1:], BF16)
    g2 = jnp.concatenate([g2_top[...], g2_end[...]], axis=0)
    copy.wait()
    stack_heads((partial[...] + dot(g2, held[...], NT)).astype(BF16), g5, rows)
    delta[...] = jnp.sum(attn_t[...].astype(F32) * g5[...].T.astype(F32), axis=0, keepdims=True)
    refs, outs = side_group(side, other, 1, stay, leave, 2)
    refs, outs = refs + beside_refs(other, core), outs + ((leave, 5), (leave, 6 - 2 * core))
    groups = [side_group(side, other, 2, stay, leave, 0), (refs, outs)]
    backward_parts(rows, factor, scale, groups, info, q5, g5, lse, delta, None, acc)


def backward_second(rows, factor, scale, info, q5, g5, lse, delta, side, other, before, acc, stay, leave):
    groups = [side_group(side, other, 3, stay, leave, 0)]
    backward_parts(rows, factor, scale, groups, info, q5, g5, lse, delta, before[...], acc)


def backward_column(
    rows, factor, scale, weight, info, q5, g5, lse, delta, column, acc, attn, dq, stay, here, held, sem
):
    x = lax.axis_index("mp")
    at = pl.multiple_of(x * held.shape[1], 128)
    copy = pltpu.make_async_copy(weight.at[:, pl.ds(at, held.shape[1])], held, sem)
    copy.start()
    width = info.shape[1]
    norm = jnp.where(info[2:3, :] > 0.5, lse[...], HIGH)
    refs = column_refs(column)
    visible = masks(refs, info, rows, width, True)
    total = acc[...]
    for part, limit in ((slice(0, 1), lse[...]), (slice(1, 3), norm)):
        d_key, d_value, d_query = grads_of(
            refs[part], visible[part], limit, delta[...], q5[...], g5[...], rows, factor, scale
        )
        for i, slot in enumerate(range(3)[part]):
            stay[slot, :, :HD] = d_key[i * rows : (i + 1) * rows]
            stay[slot, :, HD:] = d_value[i * rows : (i + 1) * rows]
        total = total + d_query
    spread_heads((total * scale).astype(BF16).T, dq, rows)
    copy.wait()
    here[...] = dot(attn[...], held[...], NN).astype(BF16)


def grad_heads(g0, g1, g3, weight, partial, held, weights, sem):
    x = lax.axis_index("mp")
    part = held.shape[2]
    order = (0, 1, 3)
    loads, copies = [], []
    for index, (back, piece) in enumerate(zip(order, (g0, g1, g3))):
        column = pl.multiple_of(lax.rem(x + NX - back, NX) * part, 128)
        source = weight.at[:, pl.ds(column, part)]
        loads.append(pltpu.make_async_copy(source, weights.at[index], sem.at[2 * index]))
        copies.append(pltpu.make_async_copy(piece, held.at[index], sem.at[2 * index + 1]))
        loads[-1].start()
        copies[-1].start()
    total = None
    for index in range(len(order)):
        loads[index].wait()
        copies[index].wait()
        term = dot(held[index], weights[index], NT)
        total = term if total is None else total + term
    partial[...] = total


def join_features(here, up, down, out):
    out[...] = (here[...].astype(F32) + up[...].astype(F32) + down[...].astype(F32)).astype(BF16)


def add_up(*terms):
    return sum(t.astype(F32) for t in terms)


def per_device(queries, keys, values, seg_ids, out_weight, grad_out):
    rows = queries.shape[0]
    scale = 1.0 / math.sqrt(HD)
    factor = scale * math.log2(math.e)
    width = -(-GROUP * rows // 128) * 128
    y, z, _ = where_am_i()
    x = lax.axis_index("mp")
    vmem = pl.BlockSpec(memory_space=pltpu.VMEM)

    def shape(*dims, dtype=BF16):
        return jax.ShapeDtypeStruct(dims, dtype)

    anywhere = pl.BlockSpec(memory_space=pl.ANY)

    fixed = pl.BlockSpec(memory_space=pltpu.HBM)

    def call(body, outs, micros, *operands, loose=0, pinned=0, scratch=(), mib=24):
        return pl.pallas_call(
            body,
            out_shape=outs,
            in_specs=[anywhere] * loose
            + [fixed] * pinned
            + [vmem] * (len(operands) - loose - pinned),
            out_specs=jax.tree.map(lambda _: vmem, outs),
            scratch_shapes=scratch,
            cost_estimate=pl.CostEstimate(flops=micros * 1_153_000_000, bytes_accessed=0, transcendentals=0),
            compiler_params=pltpu.CompilerParams(vmem_limit_bytes=mib * 1024 * 1024),
        )(*operands)

    line = shape(1, width, dtype=F32)
    square = shape(HD, width, dtype=F32)
    stacked = shape(width, HD)
    half = rows // 2

    own = call(
        pack, shape(rows + TILE, 2 * HD), 1, seg_ids.reshape(1, rows), keys, values, pinned=3, mib=60,
        scratch=[pltpu.VMEM((1, rows), jnp.int32), pltpu.SemaphoreType.DMA((3,))],
    )
    y1, y2 = move(own, dy=1), move(own, dy=2)
    g1, g3 = move_x(grad_out, 1), move_x(grad_out, 3)
    y1, y2 = lax.optimization_barrier((y1, y2))
    y1, y2 = jnp.where(y >= 1, y1, 0), jnp.where(y >= 2, y2, 0)

    column = jnp.stack([own, y1, y2])
    sides = {dz: jnp.stack([y1, jnp.where(z + dz < NZ, own, y2)]) for dz in (2, 1, 3)}
    sides = [move(sides[dz], dz=dz) for dz in (1, 2, 3)]
    g2_top, g2_end = move_x(g1[:half], 1), move_x(g3[half:], 3)
    top, total, acc, q5, info = call(
        lambda *refs: forward_column(rows, factor, *refs),
        (line, line, square, stacked, shape(8, width, dtype=F32)), 1, queries, column,
    )
    part = grad_out.shape[1]
    partial = call(
        grad_heads, shape(rows, GROUP * HD, dtype=F32), 3, grad_out, g1, g3, out_weight, loose=3, pinned=1,
        scratch=[
            pltpu.VMEM((NX - 1, rows, part), BF16),
            pltpu.VMEM((NX - 1, out_weight.shape[0], part), BF16),
            pltpu.SemaphoreType.DMA((2 * (NX - 1),)),
        ],
    )
    *sides, top, partial = lax.optimization_barrier((*sides, top, partial))

    side = jnp.concatenate([*sides, column])
    side_other = move(side, flip=1)
    top, total, acc, side_other = lax.optimization_barrier(
        (
            *call(
                lambda *refs: forward_near(rows, factor, *refs),
                (line, line, square), 4, info, q5, side, top, total, acc,
            ),
            side_other,
        )
    )
    whole, halved = shape(rows, part), shape(half, part)
    lse, attn_t, attn, up, down, *far = call(
        lambda *refs: forward_far(rows, factor, *refs),
        (line, shape(HD, width), shape(rows, GROUP * HD), whole, whole, halved, halved), 1,
        out_weight, info, q5, side_other, top, total, acc, pinned=1, mib=30,
        scratch=[pltpu.VMEM(out_weight.shape, BF16), pltpu.SemaphoreType.DMA],
    )
    lse, *far, g2_top, g2_end = lax.optimization_barrier((lse, *far, g2_top, g2_end))
    early = (move_x(far[0], 1), move_x(far[1], 3))

    def pieces(count):
        return shape(count, rows, 2 * HD)

    acc, stay, leave, g5, delta, *early = lax.optimization_barrier(
        (
            *call(
                lambda *refs: backward_first(rows, factor, scale, *refs),
                (square, pieces(4), pieces(7), stacked, line), 8,
                out_weight, info, q5, partial, g2_top, g2_end, attn_t, lse, side, side_other, pinned=1,
                scratch=[pltpu.VMEM((out_weight.shape[0], part), BF16), pltpu.SemaphoreType.DMA],
            ),
            *early,
        )
    )
    up = jnp.concatenate([add_up(up[:half], early[0]).astype(BF16), up[half:]], axis=0)
    down = jnp.concatenate([down[:half], add_up(down[half:], early[1]).astype(BF16)], axis=0)
    other = move(leave, flip=1)
    acc, other = lax.optimization_barrier((acc, other))
    acc, stay_last, leave_last = call(
        lambda *refs: backward_second(rows, factor, scale, *refs),
        (square, pieces(2), pieces(2)), 7, info, q5, g5, lse, delta, side, side_other, acc,
    )
    other_last = move(leave_last, flip=1)
    mixed = add_up(stay, other[:4]).astype(BF16)
    returned = {2: move(mixed[:2], dz=-2), 1: move(mixed[2:], dz=-1)}
    returned[3] = move(add_up(stay_last, other_last).astype(BF16), dz=-3)
    up, down = move_x(up, 1), move_x(down, 3)
    grad_query, stay, here, returned[1], returned[2], returned[3], up, down = lax.optimization_barrier(
        (
            *call(
                lambda *refs: backward_column(rows, factor, scale, *refs),
                (shape(rows, GROUP * HD), pieces(3), whole), 1,
                out_weight, info, q5, g5, lse, delta, column, acc, attn, pinned=1,
                scratch=[pltpu.VMEM((out_weight.shape[0], part), BF16), pltpu.SemaphoreType.DMA],
            ),
            returned[1], returned[2], returned[3], up, down,
        )
    )
    projected = add_up(here, up, down).astype(BF16)
    mixed = add_up(stay, other[4:])
    first, second, third = mixed[0], mixed[1], mixed[2]
    for dz in range(1, NZ):
        far, near = returned[dz][0].astype(F32), returned[dz][1].astype(F32)
        second = second + far
        first = first + jnp.where(z + dz < NZ, near, 0.0)
        third = third + jnp.where(z + dz < NZ, 0.0, near)
    second, third = second.astype(BF16), third.astype(BF16)
    grads = add_up(first, move(second, dy=-1), move(third, dy=-2)).astype(BF16)
    return (projected, grad_query, grads[:, :HD], grads[:, HD:])


def solution(mesh):
    return jax.shard_map(
        per_device,
        mesh=mesh,
        in_specs=(
            P("dp", "mp"),
            P("dp", "mp"),
            P("dp", "mp"),
            P("dp"),
            P("mp", None),
            P("dp", "mp"),
        ),
        out_specs=(P("dp", "mp"), P("dp", "mp"), P("dp", "mp"), P("dp", "mp")),
        check_vma=False,
    )
```

```python
import math

import jax
import jax.numpy as jnp
from jax import lax
from jax.experimental import pallas as pl
from jax.experimental.pallas import tpu as pltpu
from jax.sharding import PartitionSpec as P

HD = 128
GROUP = 5
NX = 4
NY = 4
NZ = 4
TILE = 16
LOW = -1e30
HIGH = 1e30
F32 = jnp.float32
BF16 = jnp.bfloat16
NT = (((1,), (1,)), ((), ()))
TN = (((0,), (0,)), ((), ()))
NN = (((1,), (0,)), ((), ()))


def place(y, z, core):
    return ((y % NY) * NZ + (z % NZ)) * 2 + core


def shift(dy, dz, flip):
    pairs = []
    for y in range(NY):
        for z in range(NZ):
            for core in range(2):
                pairs.append((place(y, z, core), place(y + dy, z + dz, core ^ flip)))
    return pairs


def move(value, dy=0, dz=0, flip=0):
    return lax.ppermute(value, "dp", shift(dy, dz, flip))


def move_x(value, dx):
    return lax.ppermute(value, "mp", [(x, (x + dx) % NX) for x in range(NX)])


def dot(a, b, dims):
    return lax.dot_general(a, b, dims, preferred_element_type=F32)


def where_am_i():
    index = lax.axis_index("dp")
    return index // (2 * NZ), (index // 2) % NZ, index % 2


def stack_heads(source, target, rows):
    for head in range(GROUP):
        target[head * rows : (head + 1) * rows, :] = source[:, head * HD : (head + 1) * HD]
    target[GROUP * rows :, :] = jnp.zeros((target.shape[0] - GROUP * rows, HD), BF16)


def spread_heads(stacked, target, rows):
    for head in range(GROUP):
        target[:, head * HD : (head + 1) * HD] = stacked[head * rows : (head + 1) * rows, :]


def joined(parts):
    return parts[0] if len(parts) == 1 else jnp.concatenate(parts, axis=0)


def seen(tile, seg, rows):
    match = jnp.sum(jnp.where(tile.astype(F32) == seg, 1.0, 0.0), axis=0, keepdims=True)
    return rows - jnp.sum(match, axis=1, keepdims=True)


def masks(refs, info, rows, width, own):
    at = lax.broadcasted_iota(jnp.int32, (rows, width), 0).astype(F32)
    result = []
    for index, (ref, slot) in enumerate(refs):
        if own and index == 0:
            segs = ref[slot, pl.ds(rows, TILE), :].astype(F32).T[:rows, :1]
            result.append((at <= info[0:1, :]) & (segs == info[1:2, :]))
        else:
            result.append(at >= seen(ref[slot, pl.ds(rows, TILE), :], info[3:4, : 2 * HD], rows))
    return result


def attend(refs, visible, norm_of, q5, rows, factor, state, seen_rows):
    keys = joined([ref[slot, pl.ds(0, rows), pl.ds(0, HD)] for ref, slot in refs])
    values = joined([ref[slot, pl.ds(0, rows), pl.ds(HD, HD)] for ref, slot in refs])
    raw = dot(keys, q5, NT)
    scores = [jnp.where(see, raw[i * rows : (i + 1) * rows], LOW) for i, see in enumerate(visible)]
    peak = jnp.max(scores[0], axis=0, keepdims=True)
    for part in scores[1:]:
        peak = jnp.maximum(peak, jnp.max(part, axis=0, keepdims=True))
    peak = peak * factor
    if seen_rows is not None:
        peak = jnp.where(seen_rows, peak, LOW)
    top, total, acc = state
    new = peak if top is None else jnp.maximum(top, peak)
    norm = new if seen_rows is None else jnp.where(seen_rows, new, HIGH)
    weights = [jnp.exp2(part * factor - norm) for part in scores]
    added = sum(jnp.sum(w, axis=0, keepdims=True) for w in weights)
    out = dot(values, joined([w.astype(BF16) for w in weights]), TN)
    if top is None:
        return new, added, out
    alpha = jnp.exp2(top - new)
    return new, total * alpha + added, acc * alpha + out


def column_refs(column):
    return [(column, 0), (column, 1), (column, 2)]


def beside_refs(other, core):
    return [(other, 2 * NZ - 1), (other, 2 * NZ - 2 * core)]


def side_refs(side, other, dz):
    return [(side, dz * 2), (other, dz * 2), (side, dz * 2 + 1), (other, dz * 2 + 1)]


def pack(seg, keys, values, own, line, sem):
    rows = keys.shape[0]
    copies = [
        pltpu.make_async_copy(seg, line, sem.at[0]),
        pltpu.make_async_copy(keys, own.at[pl.ds(0, rows), pl.ds(0, HD)], sem.at[1]),
        pltpu.make_async_copy(values, own.at[pl.ds(0, rows), pl.ds(HD, HD)], sem.at[2]),
    ]
    for copy in copies:
        copy.start()
    copies[0].wait()
    own[rows:, :] = jnp.zeros((TILE, 2 * HD), BF16)
    first = lax.broadcasted_iota(jnp.int32, (TILE, rows), 0) == 0
    own[rows:, :rows] = jnp.where(first, (line[...] + 1).astype(F32), 0.0).astype(BF16)
    copies[1].wait()
    copies[2].wait()


def describe_rows(tile, rows, info):
    width = info.shape[1]
    lane = lax.broadcasted_iota(jnp.int32, (2 * HD, width), 1)
    for head in range(1, GROUP + 1):
        lane = lane - jnp.where(lane >= rows, rows, 0)
    place_in = lax.broadcasted_iota(jnp.int32, (2 * HD, width), 0)

    def picked(at):
        return dot(tile, jnp.where(place_in == at, 1.0, 0.0).astype(BF16), NN)[:1, :]

    segs, first = picked(lane), picked(0)
    info[0:1, :] = lane[:1, :].astype(F32)
    info[1:2, :] = segs
    info[2:3, :] = jnp.where(segs == first, 1.0, 0.0)
    info[3:4, :] = first
    info[4:, :] = jnp.zeros((info.shape[0] - 4, width), F32)


def forward_column(rows, factor, q, column, top, total, acc, q5, info):
    stack_heads(q, q5, rows)
    describe_rows(column[0, pl.ds(rows, TILE), :], rows, info)
    width = info.shape[1]
    near = info[2:3, :] > 0.5
    refs = column_refs(column)
    visible = masks(refs, info, rows, width, True)
    state = attend(refs[:1], visible[:1], None, q5[...], rows, factor, (None, None, None), None)
    state = attend(refs[1:], visible[1:], None, q5[...], rows, factor, state, near)
    top[...], total[...], acc[...] = state


def forward_near(rows, factor, info, q5, side, top, total, acc, top_out, total_out, acc_out):
    near = info[2:3, :] > 0.5
    state = (top[...], total[...], acc[...])
    for group in (range(0, 3), range(3, 6)):
        refs = [(side, slot) for slot in group]
        visible = masks(refs, info, rows, info.shape[1], False)
        state = attend(refs, visible, None, q5[...], rows, factor, state, near)
    top_out[...], total_out[...], acc_out[...] = state


def forward_far(
    rows, factor, weight, info, q5, other, top, total, acc,
    lse, attn_t, attn, up, down, far_top, far_end, held, sem,
):
    copy = pltpu.make_async_copy(weight, held, sem)
    copy.start()
    x = lax.axis_index("mp")
    _, _, core = where_am_i()
    near = info[2:3, :] > 0.5
    state = (top[...], total[...], acc[...])
    shards = [(other, slot) for slot in range(2 * NZ - 2)] + beside_refs(other, core)
    for refs in (shards,):
        visible = masks(refs, info, rows, info.shape[1], False)
        state = attend(refs, visible, None, q5[...], rows, factor, state, near)
    out_t = (state[2] / state[1]).astype(BF16)
    spread_heads(out_t.T, attn, rows)
    lse[...] = state[0] + jnp.log2(state[1])
    attn_t[...] = out_t
    copy.wait()
    part = up.shape[1]

    def features(dx):
        column = pl.multiple_of(lax.rem(x + dx, NX) * part, 128)
        return dot(attn[...], held[:, pl.ds(column, part)], NN).astype(BF16)

    far = features(2)
    far_top[...] = far[: rows // 2]
    far_end[...] = far[rows // 2 :]
    up[...] = features(1)
    down[...] = features(3)


def grads_of(refs, visible, norm, delta, q5, g5, rows, factor, scale):
    keys = joined([ref[slot, pl.ds(0, rows), pl.ds(0, HD)] for ref, slot in refs])
    values = joined([ref[slot, pl.ds(0, rows), pl.ds(HD, HD)] for ref, slot in refs])
    raw = dot(keys, q5, NT)
    slope = dot(values, g5, NT)
    weights = []
    for i, see in enumerate(visible):
        part = raw[i * rows : (i + 1) * rows] * factor - norm
        weights.append(jnp.exp2(jnp.where(see, part, LOW)))
    weights = joined(weights)
    slope = (weights * (slope - delta)).astype(BF16)
    d_value = dot(weights.astype(BF16), g5, NN).astype(BF16)
    d_key = (dot(slope, q5, NN) * scale).astype(BF16)
    return d_key, d_value, dot(keys, slope, TN)


def backward_parts(rows, factor, scale, groups, info, q5, g5, lse, delta, total, acc):
    norm = jnp.where(info[2:3, :] > 0.5, lse[...], HIGH)
    for refs, outs in groups:
        visible = masks(refs, info, rows, info.shape[1], False)
        d_key, d_value, d_query = grads_of(refs, visible, norm, delta[...], q5[...], g5[...], rows, factor, scale)
        for i, (out, slot) in enumerate(outs):
            out[slot, :, :HD] = d_key[i * rows : (i + 1) * rows]
            out[slot, :, HD:] = d_value[i * rows : (i + 1) * rows]
        total = d_query if total is None else total + d_query
    acc[...] = total


def side_group(side, other, dz, stay, leave, at):
    return side_refs(side, other, dz - 1), ((stay, at), (leave, at), (stay, at + 1), (leave, at + 1))


def backward_first(
    rows, factor, scale, weight, info, q5, partial, g2_top, g2_end, attn_t, lse, side, other,
    acc, stay, leave, g5, delta, held, sem,
):
    x = lax.axis_index("mp")
    column = pl.multiple_of(lax.rem(x + 2, NX) * held.shape[1], 128)
    copy = pltpu.make_async_copy(weight.at[:, pl.ds(column, held.shape[1])], held, sem)
    copy.start()
    _, _, core = where_am_i()
    leave[4 + 2 * core] = jnp.zeros(leave.shape[1:], BF16)
    g2 = jnp.concatenate([g2_top[...], g2_end[...]], axis=0)
    copy.wait()
    stack_heads((partial[...] + dot(g2, held[...], NT)).astype(BF16), g5, rows)
    delta[...] = jnp.sum(attn_t[...].astype(F32) * g5[...].T.astype(F32), axis=0, keepdims=True)
    refs, outs = side_group(side, other, 1, stay, leave, 2)
    refs, outs = refs + beside_refs(other, core), outs + ((leave, 5), (leave, 6 - 2 * core))
    groups = [side_group(side, other, 2, stay, leave, 0), (refs, outs)]
    backward_parts(rows, factor, scale, groups, info, q5, g5, lse, delta, None, acc)


def backward_second(rows, factor, scale, info, q5, g5, lse, delta, side, other, before, acc, stay, leave):
    groups = [side_group(side, other, 3, stay, leave, 0)]
    backward_parts(rows, factor, scale, groups, info, q5, g5, lse, delta, before[...], acc)


def backward_column(
    rows, factor, scale, weight, info, q5, g5, lse, delta, column, acc, attn, dq, stay, here, held, sem
):
    x = lax.axis_index("mp")
    at = pl.multiple_of(x * held.shape[1], 128)
    copy = pltpu.make_async_copy(weight.at[:, pl.ds(at, held.shape[1])], held, sem)
    copy.start()
    width = info.shape[1]
    norm = jnp.where(info[2:3, :] > 0.5, lse[...], HIGH)
    refs = column_refs(column)
    visible = masks(refs, info, rows, width, True)
    total = acc[...]
    for part, limit in ((slice(0, 1), lse[...]), (slice(1, 3), norm)):
        d_key, d_value, d_query = grads_of(
            refs[part], visible[part], limit, delta[...], q5[...], g5[...], rows, factor, scale
        )
        for i, slot in enumerate(range(3)[part]):
            stay[slot, :, :HD] = d_key[i * rows : (i + 1) * rows]
            stay[slot, :, HD:] = d_value[i * rows : (i + 1) * rows]
        total = total + d_query
    spread_heads((total * scale).astype(BF16).T, dq, rows)
    copy.wait()
    here[...] = dot(attn[...], held[...], NN).astype(BF16)


def grad_heads(g0, g1, g3, weight, partial, held, weights, sem):
    x = lax.axis_index("mp")
    part = held.shape[2]
    order = (0, 1, 3)
    loads, copies = [], []
    for index, (back, piece) in enumerate(zip(order, (g0, g1, g3))):
        column = pl.multiple_of(lax.rem(x + NX - back, NX) * part, 128)
        source = weight.at[:, pl.ds(column, part)]
        loads.append(pltpu.make_async_copy(source, weights.at[index], sem.at[2 * index]))
        copies.append(pltpu.make_async_copy(piece, held.at[index], sem.at[2 * index + 1]))
        loads[-1].start()
        copies[-1].start()
    total = None
    for index in range(len(order)):
        loads[index].wait()
        copies[index].wait()
        term = dot(held[index], weights[index], NT)
        total = term if total is None else total + term
    partial[...] = total


def join_features(here, up, down, out):
    out[...] = (here[...].astype(F32) + up[...].astype(F32) + down[...].astype(F32)).astype(BF16)


def add_up(*terms):
    return sum(t.astype(F32) for t in terms)


def per_device(queries, keys, values, seg_ids, out_weight, grad_out):
    rows = queries.shape[0]
    scale = 1.0 / math.sqrt(HD)
    factor = scale * math.log2(math.e)
    width = -(-GROUP * rows // 128) * 128
    y, z, _ = where_am_i()
    x = lax.axis_index("mp")
    vmem = pl.BlockSpec(memory_space=pltpu.VMEM)

    def shape(*dims, dtype=BF16):
        return jax.ShapeDtypeStruct(dims, dtype)

    anywhere = pl.BlockSpec(memory_space=pl.ANY)

    fixed = pl.BlockSpec(memory_space=pltpu.HBM)

    def call(body, outs, micros, *operands, loose=0, pinned=0, scratch=(), mib=24):
        return pl.pallas_call(
            body,
            out_shape=outs,
            in_specs=[anywhere] * loose
            + [fixed] * pinned
            + [vmem] * (len(operands) - loose - pinned),
            out_specs=jax.tree.map(lambda _: vmem, outs),
            scratch_shapes=scratch,
            cost_estimate=pl.CostEstimate(flops=micros * 1_153_000_000, bytes_accessed=0, transcendentals=0),
            compiler_params=pltpu.CompilerParams(vmem_limit_bytes=mib * 1024 * 1024),
        )(*operands)

    line = shape(1, width, dtype=F32)
    square = shape(HD, width, dtype=F32)
    stacked = shape(width, HD)
    half = rows // 2

    own = call(
        pack, shape(rows + TILE, 2 * HD), 1, seg_ids.reshape(1, rows), keys, values, pinned=3, mib=60,
        scratch=[pltpu.VMEM((1, rows), jnp.int32), pltpu.SemaphoreType.DMA((3,))],
    )
    y1, y2 = move(own, dy=1), move(own, dy=2)
    g1, g3 = move_x(grad_out, 1), move_x(grad_out, 3)
    y1, y2 = lax.optimization_barrier((y1, y2))
    y1, y2 = jnp.where(y >= 1, y1, 0), jnp.where(y >= 2, y2, 0)

    column = jnp.stack([own, y1, y2])
    sides = {dz: jnp.stack([y1, jnp.where(z + dz < NZ, own, y2)]) for dz in (2, 1, 3)}
    sides = [move(sides[dz], dz=dz) for dz in (1, 2, 3)]
    g2_top, g2_end = move_x(g1[:half], 1), move_x(g3[half:], 3)
    top, total, acc, q5, info = call(
        lambda *refs: forward_column(rows, factor, *refs),
        (line, line, square, stacked, shape(8, width, dtype=F32)), 1, queries, column,
    )
    part = grad_out.shape[1]
    partial = call(
        grad_heads, shape(rows, GROUP * HD, dtype=F32), 3, grad_out, g1, g3, out_weight, loose=3, pinned=1,
        scratch=[
            pltpu.VMEM((NX - 1, rows, part), BF16),
            pltpu.VMEM((NX - 1, out_weight.shape[0], part), BF16),
            pltpu.SemaphoreType.DMA((2 * (NX - 1),)),
        ],
    )
    *sides, top, partial = lax.optimization_barrier((*sides, top, partial))

    side = jnp.concatenate([*sides, column])
    side_other = move(side, flip=1)
    top, total, acc, side_other = lax.optimization_barrier(
        (
            *call(
                lambda *refs: forward_near(rows, factor, *refs),
                (line, line, square), 4, info, q5, side, top, total, acc,
            ),
            side_other,
        )
    )
    whole, halved = shape(rows, part), shape(half, part)
    lse, attn_t, attn, up, down, *far = call(
        lambda *refs: forward_far(rows, factor, *refs),
        (line, shape(HD, width), shape(rows, GROUP * HD), whole, whole, halved, halved), 1,
        out_weight, info, q5, side_other, top, total, acc, pinned=1, mib=30,
        scratch=[pltpu.VMEM(out_weight.shape, BF16), pltpu.SemaphoreType.DMA],
    )
    lse, *far, g2_top, g2_end = lax.optimization_barrier((lse, *far, g2_top, g2_end))
    early = (move_x(far[0], 1), move_x(far[1], 3))

    def pieces(count):
        return shape(count, rows, 2 * HD)

    acc, stay, leave, g5, delta, *early = lax.optimization_barrier(
        (
            *call(
                lambda *refs: backward_first(rows, factor, scale, *refs),
                (square, pieces(4), pieces(7), stacked, line), 8,
                out_weight, info, q5, partial, g2_top, g2_end, attn_t, lse, side, side_other, pinned=1,
                scratch=[pltpu.VMEM((out_weight.shape[0], part), BF16), pltpu.SemaphoreType.DMA],
            ),
            *early,
        )
    )
    up = jnp.concatenate([add_up(up[:half], early[0]).astype(BF16), up[half:]], axis=0)
    down = jnp.concatenate([down[:half], add_up(down[half:], early[1]).astype(BF16)], axis=0)
    other = move(leave, flip=1)
    acc, stay_last, leave_last, other = lax.optimization_barrier(
        (
            *call(
                lambda *refs: backward_second(rows, factor, scale, *refs),
                (square, pieces(2), pieces(2)), 3, info, q5, g5, lse, delta, side, side_other, acc,
            ),
            other,
        )
    )
    other_last = move(leave_last, flip=1)
    mixed = add_up(stay, other[:4]).astype(BF16)
    returned = {2: move(mixed[:2], dz=-2), 1: move(mixed[2:], dz=-1)}
    returned[3] = move(add_up(stay_last, other_last).astype(BF16), dz=-3)
    up, down = move_x(up, 1), move_x(down, 3)
    grad_query, stay, here, returned[1], returned[2], returned[3], up, down = lax.optimization_barrier(
        (
            *call(
                lambda *refs: backward_column(rows, factor, scale, *refs),
                (shape(rows, GROUP * HD), pieces(3), whole), 3,
                out_weight, info, q5, g5, lse, delta, column, acc, attn, pinned=1,
                scratch=[pltpu.VMEM((out_weight.shape[0], part), BF16), pltpu.SemaphoreType.DMA],
            ),
            returned[1], returned[2], returned[3], up, down,
        )
    )
    projected = add_up(here, up, down).astype(BF16)
    mixed = add_up(stay, other[4:])
    first, second, third = mixed[0], mixed[1], mixed[2]
    for dz in range(1, NZ):
        far, near = returned[dz][0].astype(F32), returned[dz][1].astype(F32)
        second = second + far
        first = first + jnp.where(z + dz < NZ, near, 0.0)
        third = third + jnp.where(z + dz < NZ, 0.0, near)
    second, third = second.astype(BF16), third.astype(BF16)
    grads = add_up(first, move(second, dy=-1), move(third, dy=-2)).astype(BF16)
    return (projected, grad_query, grads[:, :HD], grads[:, HD:])


def solution(mesh):
    return jax.shard_map(
        per_device,
        mesh=mesh,
        in_specs=(
            P("dp", "mp"),
            P("dp", "mp"),
            P("dp", "mp"),
            P("dp"),
            P("mp", None),
            P("dp", "mp"),
        ),
        out_specs=(P("dp", "mp"), P("dp", "mp"), P("dp", "mp"), P("dp", "mp")),
        check_vma=False,
    )
```
